32 devices in a mesh: tm: 4 (over y, x), chan: 8 (over z, core).
Axes of the slice: x: 2, y: 2, z: 4, core: 2. Of those that a mesh axis runs over, the one named last changes fastest.
Arguments:
- samples: bfloat16 [128, 2, 2097152], P('chan', None, 'tm'), may hold values from -6 to 6
- delays: int32 [128, 4], P('chan', 'tm'), may hold values from 0 to 32768, as said below
- delay_phase: int32 [128, 2], P('chan'), may hold values from 0 to 4095
- fringe_rate: int32 [128], P('chan'), may hold values from -2 to 2
Outputs:
- visibility: float32 [36, 2, 16, 16, 4096], P('tm', None, None, None, 'chan')
The draws below stay inside these ranges and needn't reach their ends.
Inputs may be any that keep to these rules, and one draw needn't show every extreme that they name: `delays`: in every time block some antenna has a delay of exactly 32768.
All inputs are finite; a program needn't handle non-finite values.
Results may differ from the reference program's by a relative error of at most 0.0028.
Values may be sent and summed in bfloat16 or wider, within the bound.
No kernel may reach another device: no remote copies, remote signals or barrier semaphores. Data moves between devices by JAX's collectives and lax.ppermute only.
A program may use at most 256 MiB of HBM per device.

```python
import math
import jax
import jax.numpy as jnp
import numpy as np
from jax import lax

ANTENNA_COUNT = 128
CHANNEL_COUNT = 4096
P1 = 64
P2 = 64
BB = 16
FRAME_COUNT = 128
NB = 8
TIME_BLOCKS = 4
DMAX = 32768


def shared_delays(key):
    first_key, later_random_key = jax.random.split(key)
    drawn = jax.random.randint(first_key, (ANTENNA_COUNT, TIME_BLOCKS), 0, DMAX + 1)
    picked_antenna = jax.random.randint(later_random_key, (TIME_BLOCKS,), 0, ANTENNA_COUNT)
    picked_entry = jnp.arange(ANTENNA_COUNT)[:, None] == picked_antenna[None, :]
    return jnp.where(picked_entry, DMAX, drawn).astype(jnp.int32)


def draw_delays(key, part):
    return shared_delays(jax.random.fold_in(key, 11))


def draw_samples(key, part):
    delay_table = shared_delays(jax.random.fold_in(key, 11))
    sky_key = jax.random.fold_in(key, 23)
    noise_key = jax.random.fold_in(key, 37)
    length = TIME_BLOCKS * FRAME_COUNT * CHANNEL_COUNT
    block_len = FRAME_COUNT * CHANNEL_COUNT
    sky_wave = jax.random.truncated_normal(sky_key, -4.0, 4.0, (2, length + DMAX), jnp.float32)

    def one_antenna(antenna):
        delay_row = delay_table[antenna]
        position = jnp.arange(length, dtype=jnp.int32)
        shifted = position - delay_row[position // block_len] + DMAX
        noise = jax.random.truncated_normal(jax.random.fold_in(noise_key, antenna), -4.0, 4.0, (2, length), jnp.float32)
        return (jnp.take(sky_wave, shifted, axis=1) + noise) * 0.7
    return lax.map(one_antenna, jnp.arange(ANTENNA_COUNT, dtype=jnp.int32)).astype(jnp.bfloat16)


def set_ends(values, rng, smallest, high):
    longest = values.shape.index(max(values.shape))
    spots = []
    for shift in (0, 1):
        where = [jax.random.randint(jax.random.fold_in(rng, axis), (), 0, length) for axis, length in enumerate(values.shape)]
        where[longest] = (where[longest] + shift) % values.shape[longest]
        spots.append(tuple(where))
    return values.at[spots[0]].set(smallest).at[spots[1]].set(high)


def setup_inputs(seed: int = 0) -> dict:
    streams_of = jax.random.split(jax.random.key(seed), 5)
    samples = draw_samples(jax.random.fold_in(streams_of[4], 71), 0)
    delays = draw_delays(jax.random.fold_in(streams_of[4], 71), 0)
    delay_phase = set_ends(jax.random.randint(streams_of[2], (ANTENNA_COUNT, 2), 0, CHANNEL_COUNT), jax.random.fold_in(streams_of[2], 1), 0, CHANNEL_COUNT - 1).astype(jnp.int32)
    fringe_rate = set_ends(jax.random.randint(streams_of[3], (ANTENNA_COUNT,), -2, 3), jax.random.fold_in(streams_of[3], 1), -2, 2).astype(jnp.int32)
    return {"samples": samples, "delays": delays, "delay_phase": delay_phase, "fringe_rate": fringe_rate}


def dft_matrix(length):
    indices = jnp.arange(length, dtype=jnp.int32)
    product = indices[:, None] * indices[None, :] % length
    angle = 2.0 * math.pi / length * product.astype(jnp.float32)
    factor = 1.0 / math.sqrt(length)
    cosine = jnp.cos(angle) * factor
    sine = -jnp.sin(angle) * factor
    upper_half = jnp.concatenate([cosine, sine], axis=1)
    lower_half = jnp.concatenate([-sine, cosine], axis=1)
    return jnp.concatenate([upper_half, lower_half], axis=0).astype(jnp.bfloat16)

def channelize(taper_window):
    batch = taper_window.shape[0]
    frames = taper_window.shape[2]
    first_table = dft_matrix(P1)
    second_table = dft_matrix(P2)
    cells = taper_window.reshape(batch, 2, frames, P1, P2)
    cells = jnp.transpose(cells, (0, 2, 4, 1, 3)).reshape(-1, 2 * P1)
    section_one = jnp.dot(cells, first_table, preferred_element_type=jnp.float32)
    section_one = section_one.reshape(batch, frames, P2, 2, P1)
    product = jnp.arange(P2, dtype=jnp.int32)[:, None] * jnp.arange(P1, dtype=jnp.int32)[None, :] % CHANNEL_COUNT
    angle = 2.0 * math.pi / CHANNEL_COUNT * product.astype(jnp.float32)
    twist_cos = jnp.cos(angle)
    twist_sin = -jnp.sin(angle)
    real_part = section_one[:, :, :, 0]
    imag_part = section_one[:, :, :, 1]
    turned_real = real_part * twist_cos - imag_part * twist_sin
    turned_imag = real_part * twist_sin + imag_part * twist_cos
    turned = jnp.stack([turned_real, turned_imag], axis=3).astype(jnp.bfloat16)
    turned = jnp.transpose(turned, (0, 1, 4, 3, 2)).reshape(-1, 2 * P2)
    section_two = jnp.dot(turned, second_table, preferred_element_type=jnp.float32)
    section_two = section_two.reshape(batch, frames, P1, 2, P2)
    return jnp.transpose(section_two, (0, 3, 1, 4, 2)).reshape(batch, 2, frames, CHANNEL_COUNT)

def rotate(spectra, phase_pair, rate, first_frame):
    frames = spectra.shape[2]
    frame_ids = first_frame + jnp.arange(frames, dtype=jnp.int32)
    channels = jnp.arange(CHANNEL_COUNT, dtype=jnp.int32)
    turns = (phase_pair[:, 0][:, None, None] + rate[:, None, None] * frame_ids[None, :, None] + phase_pair[:, 1][:, None, None] * channels[None, None, :]) % CHANNEL_COUNT
    angle = 2.0 * math.pi / CHANNEL_COUNT * turns.astype(jnp.float32)
    cosine = jnp.cos(angle)
    sine = jnp.sin(angle)
    real_part = spectra[:, 0]
    imag_part = spectra[:, 1]
    out_real = real_part * cosine + imag_part * sine
    out_imag = imag_part * cosine - real_part * sine
    return jnp.stack([out_real, out_imag], axis=1).astype(jnp.bfloat16)

def pair_tables(tiles):
    upper_list = []
    lower_list = []
    for upper_tile in range(tiles):
        for lower_tile in range(upper_tile, tiles):
            upper_list.append(upper_tile)
            lower_list.append(lower_tile)
    return (np.array(upper_list, np.int32), np.array(lower_list, np.int32))

def reference(samples, delays, delay_phase, fringe_rate):
    block_len = FRAME_COUNT * CHANNEL_COUNT

    def one_antenna(inputs):
        stream, delay_row, phase_pair, rate = inputs
        padded = jnp.concatenate([stream, jnp.zeros((2, DMAX), stream.dtype)], axis=1)
        pieces = []
        for number in range(TIME_BLOCKS):
            begin = (number * block_len + delay_row[number]).astype(jnp.int32)
            pieces.append(lax.dynamic_slice_in_dim(padded, begin, block_len, 1))
        taper_window = jnp.concatenate(pieces, axis=1).reshape(1, 2, TIME_BLOCKS * FRAME_COUNT, CHANNEL_COUNT)
        spectra = channelize(taper_window)
        return rotate(spectra, phase_pair[None], rate.reshape(1), jnp.int32(0))[0]
    rotated = lax.map(one_antenna, (samples, delays, delay_phase, fringe_rate))
    tiled = rotated.reshape(NB, BB, 2, TIME_BLOCKS * FRAME_COUNT, CHANNEL_COUNT)
    upper_tab, lower_tab = pair_tables(NB)
    factor = 1.0 / (FRAME_COUNT * TIME_BLOCKS)

    def one_pair(pair):
        left_tile = tiled[pair[0]].astype(jnp.float32)
        right_tile = tiled[pair[1]].astype(jnp.float32)
        swapped = jnp.stack([left_tile[:, 1], -left_tile[:, 0]], axis=1)
        real_sum = jnp.einsum('icgk,jcgk->ijk', left_tile, right_tile)
        imag_sum = jnp.einsum('icgk,jcgk->ijk', swapped, right_tile)
        return jnp.stack([real_sum, imag_sum], axis=0) * factor
    pair_list = jnp.stack([jnp.asarray(upper_tab), jnp.asarray(lower_tab)], axis=1)
    return lax.map(one_pair, pair_list)
```

```python
import functools
import math

import jax
import jax.numpy as jnp
import numpy as np
from jax import lax
from jax.experimental import pallas as pl
from jax.experimental.pallas import tpu as pltpu
from jax.sharding import PartitionSpec as P

CHANNEL_COUNT = 4096
P1 = 64
P2 = 64
BB = 16
FRAME_COUNT = 128
NB = 8
PAIRS = 36
DMAX = 32768

LANES = 128
HALF = FRAME_COUNT // 2
ROWS = HALF * CHANNEL_COUNT // LANES
RAW_ROWS = ROWS + DMAX // LANES
KB = 16
BLOCKS = P1 // KB
FG = 4


def host_dft(length):
    index = np.arange(length)
    angle = 2.0 * math.pi / length * (np.outer(index, index) % length)
    cosine = np.cos(angle) / math.sqrt(length)
    sine = -np.sin(angle) / math.sqrt(length)
    upper = np.concatenate([cosine, sine], axis=1)
    lower = np.concatenate([-sine, cosine], axis=1)
    return np.concatenate([upper, lower], axis=0).astype(np.float32)


def first_tables():
    table = host_dft(P1).reshape(2, P1 // 2, 2, 2, BLOCKS, KB)
    return table.transpose(4, 2, 3, 5, 1, 0).reshape(BLOCKS, 4 * KB, P1)


def second_table():
    return host_dft(P2).T


def turn_factors(turns):
    angle = 2.0 * math.pi / CHANNEL_COUNT * (turns % CHANNEL_COUNT).astype(jnp.float32)
    return jnp.cos(angle), jnp.sin(angle)


def twist_tables(slopes):
    product = np.outer(np.arange(P1), np.arange(P2)) % CHANNEL_COUNT
    angle = 2.0 * math.pi / CHANNEL_COUNT * product
    twist_cos = np.cos(angle).astype(np.float32)
    twist_sin = -np.sin(angle).astype(np.float32)
    cosine, sine = turn_factors(slopes[:, None] * jnp.arange(P1, dtype=jnp.int32)[None, :])
    cosine, sine = cosine[:, :, None], sine[:, :, None]
    real = twist_cos * cosine + twist_sin * sine
    imag = twist_sin * cosine - twist_cos * sine
    return jnp.concatenate([real, imag], axis=2), jnp.concatenate([-imag, real], axis=2)


def fringe_tables(delay_phase, fringe_rate, first_frame):
    antennas = fringe_rate.shape[0]
    frames = first_frame + jnp.arange(HALF, dtype=jnp.int32)
    lanes = delay_phase[:, 0][:, None] + fringe_rate[:, None] * frames[None, :]
    rows = P1 * jnp.arange(P2, dtype=jnp.int32)
    turns = lanes.reshape(antennas // 2, 1, 2, HALF) + (
        delay_phase[:, 1].reshape(antennas // 2, 1, 2, 1) * rows[None, :, None, None]
    )
    return turn_factors(turns.reshape(antennas // 2, P2, 2 * HALF))


def spectra_kernel(
    antennas, sources, waits, carried, start_ref, rest_ref, me_ref, *rest
):
    rest = rest[waits + carried:]
    devices = NB
    sample_refs = rest[: len(sources)]
    first_ref, second_ref, twist_a_ref, twist_b_ref, cos_ref, sin_ref = rest[len(sources):][:6]
    outs = rest[len(sources) + 6:][:devices]
    raw, turned, spread, sems = rest[len(sources) + 6 + devices + carried:]

    def fetches(antenna, slot):
        copies = []
        place = 0
        for number, (begin, count) in enumerate(sources):
            copies.append(pltpu.make_async_copy(
                sample_refs[number].at[antenna, pl.ds(begin, count)],
                raw.at[slot, pl.ds(place, count)],
                sems.at[slot, number],
            ))
            place += count
        return copies

    for copy in fetches(0, 0):
        copy.start()
    raw[:, RAW_ROWS:] = jnp.zeros((2, 8, 2, LANES), raw.dtype)
    lane = lax.broadcasted_iota(jnp.int32, (1, LANES), 1)

    def one_antenna(antenna, carry):
        slot = lax.rem(antenna, 2)

        @pl.when(antenna + 1 < antennas)
        def _():
            for copy in fetches(antenna + 1, 1 - slot):
                copy.start()

        for copy in fetches(antenna, slot):
            copy.wait()
        begin = start_ref[antenna]
        shift = rest_ref[antenna]
        later = (lane < shift).astype(jnp.float32)
        take_later = jnp.broadcast_to(later, (16, LANES)).astype(jnp.bfloat16)
        take_now = jnp.broadcast_to(1.0 - later, (16, LANES)).astype(jnp.bfloat16)
        take_later = jnp.concatenate([take_later] * (FG * 4), axis=0)
        take_now = jnp.concatenate([take_now] * (FG * 4), axis=0)
        odd = ((lane - shift) & (LANES - 1)) >= P2
        odd = jnp.broadcast_to(odd, (FG * KB, LANES))
        turn_one = (LANES - shift) & (LANES - 1)
        turn_two = (P2 - shift) & (LANES - 1)
        twist_a = jnp.concatenate([twist_a_ref[antenna]] * FG, axis=0)
        twist_b = jnp.concatenate([twist_b_ref[antenna]] * FG, axis=0)
        table = first_ref[0]

        def some_frames(step, carry):
            row = begin + step * (FG * 32)
            now = raw[slot, pl.ds(row, FG * 32)].reshape(FG * 64, LANES)
            next_row = raw[slot, pl.ds(row + 1, FG * 32)].reshape(FG * 64, LANES)
            cells = now * take_now + next_row * take_later
            parts_of = [[], [], [], []]
            for pair in range(FG // 2):
                both = jnp.concatenate(
                    [cells[pair * 128: pair * 128 + 64], cells[pair * 128 + 64: pair * 128 + 128]],
                    axis=1,
                )
                product = jnp.dot(table, both, preferred_element_type=jnp.float32)
                for frame in range(2):
                    for part in range(4):
                        parts_of[part].append(
                            product[part * KB:(part + 1) * KB, frame * LANES:(frame + 1) * LANES]
                        )
            even_re, even_im, odd_re, odd_im = [jnp.concatenate(p, axis=0) for p in parts_of]
            real = jnp.where(odd, odd_re, even_re)
            imag = jnp.where(odd, odd_im, even_im)
            real = pltpu.roll(real, turn_one, 1) + pltpu.roll(real, turn_two, 1)
            imag = pltpu.roll(imag, turn_one, 1) + pltpu.roll(imag, turn_two, 1)
            place = pl.multiple_of((antenna * HALF + step * FG) * KB, FG * KB)
            turned[pl.ds(place, FG * KB), :] = real * twist_a + imag * twist_b
            return carry

        lax.fori_loop(0, HALF // FG, some_frames, 0, unroll=4)
        return carry

    lax.fori_loop(0, antennas, one_antenna, 0)

    second = second_ref[...]
    low = jnp.broadcast_to(lane < HALF, (P2, LANES))

    def one_channel(k1, carry):
        for group in range(antennas // 4):
            rows = turned[pl.ds(group * 4 * HALF * KB + k1, 4 * HALF, stride=KB), :]
            spectra = lax.dot_general(
                second, rows.astype(jnp.bfloat16), (((1,), (1,)), ((), ())),
                preferred_element_type=jnp.float32,
            )
            for pair in range(2):
                real = spectra[:P2, pair * LANES:(pair + 1) * LANES]
                imag = spectra[P2:, pair * LANES:(pair + 1) * LANES]
                cosine = cos_ref[group * 2 + pair]
                sine = sin_ref[group * 2 + pair]
                out_real = real * cosine + imag * sine
                out_imag = imag * cosine - real * sine
                antenna = group * 4 + pair * 2
                spread[pl.ds(antenna, P2, stride=antennas), :] = jnp.where(
                    low, out_real, pltpu.roll(out_imag, HALF, 1)
                )
                spread[pl.ds(antenna + 1, P2, stride=antennas), :] = jnp.where(
                    low, pltpu.roll(out_real, HALF, 1), out_imag
                )
        width = P2 // devices
        for step in range(devices):
            target = step ^ me_ref[0]
            place = pl.multiple_of(target * (width * antennas), width * antennas)
            block = spread[pl.ds(place, width * antennas), :].astype(jnp.bfloat16)
            block = block.reshape(width, antennas, LANES)
            outs[step][:, k1] = block
        return carry

    lax.fori_loop(0, KB, one_channel, 0)


def spectra_call(samples, sources, start, rest, me, tables, block, after, carry):
    first, second, twist_a, twist_b, cosine, sine = tables
    antennas = start.shape[0]
    width = P2 // NB
    shape = jax.ShapeDtypeStruct((width, KB, antennas, LANES), jnp.bfloat16)
    grid_spec = pltpu.PrefetchScalarGridSpec(
        num_scalar_prefetch=3,
        grid=(1,),
        in_specs=[pl.BlockSpec(memory_space=pl.ANY) for _ in (*after, *carry, *sources)] + [
            pl.BlockSpec((1, 4 * KB, P1), lambda i, *_: (block, 0, 0)),
            pl.BlockSpec((2 * P2, 2 * P2), lambda i, *_: (0, 0)),
            pl.BlockSpec((antennas, KB, LANES), lambda i, *_: (0, block, 0)),
            pl.BlockSpec((antennas, KB, LANES), lambda i, *_: (0, block, 0)),
            pl.BlockSpec((antennas // 2, P2, LANES), lambda i, *_: (0, 0, 0)),
            pl.BlockSpec((antennas // 2, P2, LANES), lambda i, *_: (0, 0, 0)),
        ],
        out_specs=[
            pl.BlockSpec((width, KB, antennas, LANES), lambda i, *_: (0, 0, 0, 0))
            for _ in range(NB)
        ] + [pl.BlockSpec(memory_space=pl.ANY) for _ in carry],
        scratch_shapes=[
            pltpu.VMEM((2, RAW_ROWS + 8, 2, LANES), jnp.bfloat16),
            pltpu.VMEM((antennas * HALF * KB, LANES), jnp.float32),
            pltpu.VMEM((P2 * antennas, LANES), jnp.float32),
            pltpu.SemaphoreType.DMA((2, len(sources))),
        ],
    )
    outs = pl.pallas_call(
        functools.partial(spectra_kernel, antennas, sources, len(after), len(carry)),
        grid_spec=grid_spec,
        out_shape=[shape] * NB + [shape] * len(carry),
        input_output_aliases={3 + len(after) + i: NB + i for i in range(len(carry))},
        compiler_params=pltpu.CompilerParams(vmem_limit_bytes=48 << 20),
        cost_estimate=pl.CostEstimate(
            flops=300_000_000_000, bytes_accessed=30_000_000, transcendentals=0
        ),
        name="spectra",
    )(start, rest, me, *after, *carry, *samples, first, second, twist_a, twist_b, cosine, sine)
    return outs[:NB], outs[NB:]


def power_kernel(waits, carried, me_ref, *rest):
    rest = rest[waits + carried:]
    halves = (rest[:NB], rest[NB: 2 * NB])
    out = rest[2 * NB]
    cells, power = rest[2 * NB + 1 + carried:]
    step = pl.program_id(0)
    antennas = BB * NB
    for half in range(2):
        for source in range(NB):
            place = pl.multiple_of((source ^ me_ref[0]) * BB, BB)
            cells[:, pl.ds(place, BB), half * LANES:(half + 1) * LANES] = halves[half][source][0]

    lane = lax.broadcasted_iota(jnp.int32, (antennas, LANES), 1)
    low = lane < HALF

    def swap(value):
        wide = pltpu.roll(value.astype(jnp.float32), HALF, 1)
        return jnp.where(low, wide, -wide).astype(jnp.bfloat16)

    def one_channel(k, carry):
        right = cells[k]
        left = jnp.concatenate(
            [right, jnp.concatenate([swap(right[:, :LANES]), swap(right[:, LANES:])], axis=1)],
            axis=0,
        )
        product = lax.dot_general(
            left, right, (((1,), (1,)), ((), ())), preferred_element_type=jnp.float32
        )
        place = pl.multiple_of((step * KB + k) * (2 * antennas), 2 * antennas)
        power[pl.ds(place, 2 * antennas), :] = product
        return carry

    lax.fori_loop(0, KB, one_channel, 0, unroll=2)

    @pl.when(step == pl.num_programs(0) - 1)
    def _():
        first = 0
        for upper in range(NB):
            def one_row(i, carry):
                for part in range(2):
                    row = part * antennas + upper * BB + i
                    grid = power[pl.ds(row, LANES, stride=2 * antennas), :]
                    turned = jnp.transpose(grid)
                    for lower in range(upper, NB):
                        out[first + lower - upper, part, i] = turned[
                            lower * BB:(lower + 1) * BB
                        ].astype(out.dtype)
                return carry

            lax.fori_loop(0, BB, one_row, 0)
            first += NB - upper


def power_call(me, early, late, dtype, after, carry):
    antennas = BB * NB
    width = P2 // NB
    grid_spec = pltpu.PrefetchScalarGridSpec(
        num_scalar_prefetch=1,
        grid=(width,),
        in_specs=[pl.BlockSpec(memory_space=pl.ANY) for _ in (*after, *carry)] + [
            pl.BlockSpec((1, KB, BB, LANES), lambda i, *_: (i, 0, 0, 0)) for _ in range(2 * NB)
        ],
        out_specs=[pl.BlockSpec((PAIRS, 2, BB, BB, LANES), lambda i, *_: (0, 0, 0, 0, 0))]
        + [pl.BlockSpec(memory_space=pl.ANY) for _ in carry],
        scratch_shapes=[
            pltpu.VMEM((KB, antennas, 2 * LANES), jnp.bfloat16),
            pltpu.VMEM((LANES * 2 * antennas, LANES), jnp.float32),
        ],
    )
    outs = pl.pallas_call(
        functools.partial(power_kernel, len(after), len(carry)),
        grid_spec=grid_spec,
        out_shape=[jax.ShapeDtypeStruct((PAIRS, 2, BB, BB, LANES), dtype)]
        + [jax.ShapeDtypeStruct(piece.shape, piece.dtype) for piece in carry],
        input_output_aliases={1 + len(after) + i: 1 + i for i in range(len(carry))},
        compiler_params=pltpu.CompilerParams(vmem_limit_bytes=54 << 20),
        cost_estimate=pl.CostEstimate(
            flops=300_000_000_000, bytes_accessed=30_000_000, transcendentals=0
        ),
        name="power",
    )(me, *after, *carry, *early, *late)
    return outs[0], outs[1:]


def merge_kernel(factor, *refs):
    pieces, out = refs[:-1], refs[-1]
    values = [ref[...] for ref in pieces[: BLOCKS - 1]]
    last = pieces[BLOCKS - 1][...].astype(jnp.float32)
    for ref in pieces[BLOCKS:]:
        last = last + ref[...].astype(jnp.float32)
    values.append(last)
    values = [value * factor for value in values]
    lane = lax.broadcasted_iota(jnp.int32, values[0].shape, 1)
    per_tile = LANES // P1
    for tile in range(out.shape[1] // LANES):
        total = jnp.zeros_like(values[0])
        for part in range(per_tile):
            for block in range(BLOCKS):
                target = part * P1 + block * KB
                source = (tile * per_tile + part) * KB
                moved = pltpu.roll(values[block], (target - source) % LANES, 1)
                total = jnp.where((lane >= target) & (lane < target + KB), moved, total)
        out[:, tile * LANES:(tile + 1) * LANES] = total


def merge_call(pieces, factor, own):
    rows = own * 2 * BB * BB
    flat = [piece.reshape(rows, LANES) for piece in pieces]
    step = 2 * BB * BB
    channels = (P2 // NB) * P1
    merged = pl.pallas_call(
        functools.partial(merge_kernel, factor),
        grid=(own,),
        in_specs=[pl.BlockSpec((step, LANES), lambda i: (i, 0)) for _ in flat],
        out_specs=pl.BlockSpec((step, channels), lambda i: (i, 0)),
        out_shape=jax.ShapeDtypeStruct((rows, channels), jnp.float32),
        compiler_params=pltpu.CompilerParams(vmem_limit_bytes=32 << 20),
        cost_estimate=pl.CostEstimate(
            flops=1_000_000_000, bytes_accessed=20_000_000, transcendentals=0
        ),
        name="merge",
    )(*flat)
    return merged.reshape(own, 2, BB, BB, channels)


def send(value, step):
    if step == 0:
        return value
    return lax.ppermute(value, "chan", [(i, i ^ step) for i in range(NB)])


def prepare(samples, delays):
    antennas, _, length = samples.shape
    rows = samples.reshape(antennas, 2, length // LANES, LANES).transpose(0, 2, 1, 3)
    delay = delays[:, 0]
    return rows, delay // LANES, delay % LANES


SEND_ORDER = (4, 6, 2, 5, 7, 3, 1, 0)
DEPARTURES = (5, 4, 5, 5, 5, 4, 5, 5, 4, 5, 9)


def fast_body(samples, delays, delay_phase, fringe_rate):
    groups = lax.axis_size("tm")
    rows, start, rest = prepare(samples, delays)
    spill = lax.ppermute(
        rows[:, : DMAX // LANES], "tm", [(i + 1, i) for i in range(groups - 1)]
    )
    me = lax.axis_index("chan").astype(jnp.int32).reshape(1)
    twist_a, twist_b = twist_tables(delay_phase[:, 1])
    first = jnp.asarray(first_tables(), jnp.bfloat16)
    second = jnp.asarray(second_table(), jnp.bfloat16)
    first_frame = lax.axis_index("tm") * FRAME_COUNT
    tables = [first, second, twist_a, twist_b]
    early_tables = tables + list(fringe_tables(delay_phase, fringe_rate, first_frame))
    late_tables = tables + list(fringe_tables(delay_phase, fringe_rate, first_frame + HALF))

    sources = (
        ((rows,), ((0, RAW_ROWS),), early_tables),
        ((rows, spill), ((ROWS, ROWS), (0, DMAX // LANES)), late_tables),
    )
    own = PAIRS // groups
    place = lax.axis_index("tm")

    order = [("spectra", 0), ("spectra", 1)]
    for block in range(1, BLOCKS):
        order += [("spectra", 2 * block), ("spectra", 2 * block + 1), ("power", block - 1)]
    order.append(("power", BLOCKS - 1))
    parts = [(half, step) for half in range(2 * BLOCKS) for step in SEND_ORDER if step]
    departs = {}
    queue = list(parts)
    for slot, count in enumerate(DEPARTURES):
        for part in queue[:count]:
            departs[part] = slot
        queue = queue[count:]

    made, got, results = {}, {}, []
    previous = []
    for slot, (kind, number) in enumerate(order):
        waiting = [part for part in parts if departs[part] == slot and part in made]
        carry = [made[part] for part in waiting]
        arrived = [got[part] for part in parts if departs[part] == slot - 2]
        previous = previous + arrived
        if kind == "spectra":
            arrays, spans, half_tables = sources[number % 2]
            pieces, carried = spectra_call(
                arrays, spans, start, rest, me, half_tables, number // 2, previous, carry
            )
            for step in range(NB):
                made[number, step] = pieces[step]
            got[number, 0] = pieces[0]
            previous = [pieces[0]]
        else:
            last = number == BLOCKS - 1
            halves = [[got[2 * number + half, step] for step in range(NB)] for half in range(2)]
            power, carried = power_call(
                me, *halves, jnp.bfloat16 if last else jnp.float32, previous, carry
            )
            previous = [power]
        made.update(zip(waiting, carried))
        for part in parts:
            if departs[part] == slot:
                got[part] = send(made[part], part[1])
        if kind == "power" and not last:
            results.append(lax.psum_scatter(power, "tm", scatter_dimension=0, tiled=True))
    for step in range(groups):
        part = lax.dynamic_slice_in_dim(power, (place ^ step) * own, own, 0)
        if step:
            part = lax.ppermute(part, "tm", [(i, i ^ step) for i in range(groups)])
        results.append(part)
    return merge_call(results, 1.0 / (FRAME_COUNT * groups), own)


def from_behind(value, axis, by):
    devices = lax.axis_size(axis)
    pairs = [(i, i + by) for i in range(devices) if 0 <= i + by < devices]
    return lax.ppermute(value, axis, pairs)


def dft_matrix(length):
    indices = jnp.arange(length, dtype=jnp.int32)
    product = indices[:, None] * indices[None, :] % length
    angle = 2.0 * math.pi / length * product.astype(jnp.float32)
    factor = 1.0 / math.sqrt(length)
    cosine = jnp.cos(angle) * factor
    sine = -jnp.sin(angle) * factor
    upper_half = jnp.concatenate([cosine, sine], axis=1)
    lower_half = jnp.concatenate([-sine, cosine], axis=1)
    return jnp.concatenate([upper_half, lower_half], axis=0).astype(jnp.bfloat16)


def channelize(taper_window):
    batch = taper_window.shape[0]
    frames = taper_window.shape[2]
    first_table = dft_matrix(P1).reshape(2, P1, 2, P1)
    second_table = dft_matrix(P2).reshape(2, P2, 2, P2)
    cells = taper_window.reshape(batch, 2, frames, P1, P2)
    section_one = jnp.einsum(
        "acfmn,cmdk->afdkn", cells, first_table, preferred_element_type=jnp.float32
    )
    product = (
        jnp.arange(P1, dtype=jnp.int32)[:, None]
        * jnp.arange(P2, dtype=jnp.int32)[None, :]
        % CHANNEL_COUNT
    )
    angle = 2.0 * math.pi / CHANNEL_COUNT * product.astype(jnp.float32)
    twist_cos = jnp.cos(angle)
    twist_sin = -jnp.sin(angle)
    real_part = section_one[:, :, 0]
    imag_part = section_one[:, :, 1]
    turned_real = real_part * twist_cos - imag_part * twist_sin
    turned_imag = real_part * twist_sin + imag_part * twist_cos
    turned = jnp.stack([turned_real, turned_imag], axis=2).astype(jnp.bfloat16)
    section_two = jnp.einsum(
        "afdkn,dnem->aefmk", turned, second_table, preferred_element_type=jnp.float32
    )
    return section_two.reshape(batch, 2, frames, CHANNEL_COUNT)


def rotate(spectra, phase_pair, rate, first_frame):
    frames = spectra.shape[2]
    frame_ids = first_frame + jnp.arange(frames, dtype=jnp.int32)
    channels = jnp.arange(CHANNEL_COUNT, dtype=jnp.int32)
    turns = (
        phase_pair[:, 0][:, None, None]
        + rate[:, None, None] * frame_ids[None, :, None]
        + phase_pair[:, 1][:, None, None] * channels[None, None, :]
    ) % CHANNEL_COUNT
    angle = 2.0 * math.pi / CHANNEL_COUNT * turns.astype(jnp.float32)
    cosine = jnp.cos(angle)
    sine = jnp.sin(angle)
    real_part = spectra[:, 0]
    imag_part = spectra[:, 1]
    out_real = real_part * cosine + imag_part * sine
    out_imag = imag_part * cosine - real_part * sine
    return jnp.stack([out_real, out_imag], axis=1).astype(jnp.bfloat16)


def pair_tables(tiles):
    upper_list = []
    lower_list = []
    for upper_tile in range(tiles):
        for lower_tile in range(upper_tile, tiles):
            upper_list.append(upper_tile)
            lower_list.append(lower_tile)
    return (np.array(upper_list, np.int32), np.array(lower_list, np.int32))


def cross_terms(left, right):
    return jnp.einsum("tagh,tbgh->hab", left, right, preferred_element_type=jnp.float32)


def raw_power(stacked):
    real_in = stacked[:, :, 0]
    imag_in = stacked[:, :, 1]
    real_sum = cross_terms(real_in, real_in) + cross_terms(imag_in, imag_in)
    imag_sum = cross_terms(imag_in, real_in) - cross_terms(real_in, imag_in)
    return jnp.stack([real_sum, imag_sum], axis=0)


def cut_pairs(power):
    width = power.shape[1]
    upper_tab, lower_tab = pair_tables(NB)
    blocked = power.reshape(2, width, NB, BB, NB, BB)
    picked_entry = blocked[:, :, upper_tab, :, lower_tab, :]
    return jnp.transpose(picked_entry, (0, 1, 3, 4, 2))


def plain_body(samples, delays, delay_phase, fringe_rate):
    resident_antenna = samples.shape[0]
    block_len = samples.shape[2]
    spill = from_behind(samples[:, :, :DMAX], "tm", -1)
    extended = jnp.concatenate([samples, spill], axis=2)
    taper_window = jax.vmap(
        lambda stream, offset: lax.dynamic_slice_in_dim(stream, offset, block_len, 1)
    )(extended, delays[:, 0])
    taper_window = taper_window.reshape(resident_antenna, 2, FRAME_COUNT, CHANNEL_COUNT)
    spectra = channelize(taper_window)
    rotated = rotate(spectra, delay_phase, fringe_rate, lax.axis_index("tm") * FRAME_COUNT)
    group_total = lax.axis_size("tm")
    factor = 1.0 / (FRAME_COUNT * group_total)
    own_rows = PAIRS // group_total
    channel_major = lax.all_to_all(rotated, "chan", split_axis=3, concat_axis=0, tiled=True)
    all_pairs = cut_pairs(raw_power(channel_major[None])) * factor
    return lax.psum_scatter(
        lax.slice_in_dim(all_pairs, 0, own_rows * lax.axis_size("tm"), axis=0),
        "tm",
        scatter_dimension=0,
        tiled=True,
    )


def body(samples, delays, delay_phase, fringe_rate):
    fits = samples.shape[0] == BB and lax.axis_size("chan") == NB
    whole = samples.shape[2] == FRAME_COUNT * CHANNEL_COUNT and PAIRS % lax.axis_size("tm") == 0
    chosen = fast_body if fits and whole else plain_body
    return chosen(samples, delays, delay_phase, fringe_rate)


def solution(mesh):
    in_specs = (P("chan", None, "tm"), P("chan", "tm"), P("chan", None), P("chan"))
    out_specs = P("tm", None, None, None, "chan")
    return jax.shard_map(body, mesh=mesh, in_specs=in_specs, out_specs=out_specs, check_vma=False)
```

```python
import functools
import math

import jax
import jax.numpy as jnp
import numpy as np
from jax import lax
from jax.experimental import pallas as pl
from jax.experimental.pallas import tpu as pltpu
from jax.sharding import PartitionSpec as P

CHANNEL_COUNT = 4096
P1 = 64
P2 = 64
BB = 16
FRAME_COUNT = 128
NB = 8
PAIRS = 36
DMAX = 32768

LANES = 128
HALF = FRAME_COUNT // 2
ROWS = 2 * HALF * CHANNEL_COUNT // LANES
SPILL_ROWS = 2 * DMAX // LANES
RAW_ROWS = ROWS + SPILL_ROWS
FRAME_ROWS = 2 * CHANNEL_COUNT // LANES
STEP_ROWS = 16
KB = 16
BLOCKS = P1 // KB
FG = 8
UN = 8


def host_dft(length):
    index = np.arange(length)
    angle = 2.0 * math.pi / length * (np.outer(index, index) % length)
    cosine = np.cos(angle) / math.sqrt(length)
    sine = -np.sin(angle) / math.sqrt(length)
    upper = np.concatenate([cosine, sine], axis=1)
    lower = np.concatenate([-sine, cosine], axis=1)
    return np.concatenate([upper, lower], axis=0).astype(np.float32)


def first_tables():
    table = host_dft(P1).reshape(2, P1 // 2, 2, 2, BLOCKS, KB)
    table = table.transpose(4, 2, 3, 5, 1, 0).reshape(BLOCKS, 4 * KB, P1)
    return np.pad(table, ((0, 0), (0, 0), (0, LANES - P1)))


def second_table():
    return host_dft(P2).T


def turn_factors(turns):
    angle = 2.0 * math.pi / CHANNEL_COUNT * (turns % CHANNEL_COUNT).astype(jnp.float32)
    return jnp.cos(angle), jnp.sin(angle)


def twist_tables(slopes):
    product = np.outer(np.arange(P1), np.arange(P2)) % CHANNEL_COUNT
    angle = 2.0 * math.pi / CHANNEL_COUNT * product
    twist_cos = np.cos(angle).astype(np.float32)
    twist_sin = -np.sin(angle).astype(np.float32)
    cosine, sine = turn_factors(slopes[:, None] * jnp.arange(P1, dtype=jnp.int32)[None, :])
    cosine, sine = cosine[:, :, None], sine[:, :, None]
    real = twist_cos * cosine + twist_sin * sine
    imag = twist_sin * cosine - twist_cos * sine
    return jnp.concatenate([real, imag], axis=2), jnp.concatenate([-imag, real], axis=2)


def fringe_tables(delay_phase, fringe_rate, first_frame):
    antennas = fringe_rate.shape[0]
    frames = first_frame + jnp.arange(HALF, dtype=jnp.int32)
    lanes = delay_phase[:, 0][:, None] + fringe_rate[:, None] * frames[None, :]
    rows = P1 * jnp.arange(P2, dtype=jnp.int32)
    turns = lanes.reshape(antennas // 2, 1, 2, HALF) + (
        delay_phase[:, 1].reshape(antennas // 2, 1, 2, 1) * rows[None, :, None, None]
    )
    return turn_factors(turns.reshape(antennas // 2, P2, 2 * HALF))


def spectra_kernel(
    antennas, sources, waits, carried, start_ref, rest_ref, me_ref, *rest
):
    rest = rest[waits + carried:]
    devices = NB
    sample_refs = rest[: len(sources)]
    first_ref, second_ref, twist_a_ref, twist_b_ref, cos_ref, sin_ref = rest[len(sources):][:6]
    outs = rest[len(sources) + 6:][:devices]
    raw, turned, spread, sems = rest[len(sources) + 6 + devices + carried:]

    def fetches(antenna, slot):
        copies = []
        place = 0
        for number, (begin, count) in enumerate(sources):
            copies.append(pltpu.make_async_copy(
                sample_refs[number].at[antenna, pl.ds(begin, count)],
                raw.at[slot, pl.ds(place, count)],
                sems.at[slot, number],
            ))
            place += count
        return copies

    for copy in fetches(0, 0):
        copy.start()
    raw[:, RAW_ROWS:] = jnp.zeros((2, STEP_ROWS, LANES), raw.dtype)
    lane = lax.broadcasted_iota(jnp.int32, (1, LANES), 1)

    def one_antenna(antenna, carry):
        slot = lax.rem(antenna, 2)

        @pl.when(antenna + 1 < antennas)
        def _():
            for copy in fetches(antenna + 1, 1 - slot):
                copy.start()

        for copy in fetches(antenna, slot):
            copy.wait()
        begin = pl.multiple_of(start_ref[antenna] // (STEP_ROWS // 2) * STEP_ROWS, STEP_ROWS)
        extra = 2 * lax.rem(start_ref[antenna], STEP_ROWS // 2)
        table = first_ref[0].astype(jnp.float32)
        table = jnp.concatenate(
            [pltpu.roll(table, extra, 1), pltpu.roll(table, extra + 2, 1)], axis=0
        ).astype(jnp.bfloat16)[:, :FRAME_ROWS + STEP_ROWS]
        shift = rest_ref[antenna]
        later = jnp.broadcast_to(lane < shift, (4 * KB, LANES))
        odd = jnp.broadcast_to(((lane - shift) & (LANES - 1)) >= P2, (2 * KB, LANES))
        turn_one = (LANES - shift) & (LANES - 1)
        turn_two = (P2 - shift) & (LANES - 1)
        twist_a = twist_a_ref[antenna]
        twist_b = twist_b_ref[antenna]

        def some_frames(step, carry):
            for pair in range(FG // 2):
                number = step * FG + 2 * pair
                row = pl.multiple_of(begin + number * FRAME_ROWS, STEP_ROWS)
                rows = raw[slot, pl.ds(row, 2 * FRAME_ROWS + STEP_ROWS), :]
                both = jnp.concatenate(
                    [rows[:FRAME_ROWS + STEP_ROWS], rows[FRAME_ROWS:]], axis=1
                )
                product = jnp.dot(table, both, preferred_element_type=jnp.float32)
                for frame in range(2):
                    part = product[:, frame * LANES:(frame + 1) * LANES]
                    part = jnp.where(later, part[4 * KB:], part[:4 * KB])
                    part = jnp.where(odd, part[2 * KB:], part[:2 * KB])
                    part = pltpu.roll(part, turn_one, 1) + pltpu.roll(part, turn_two, 1)
                    place = pl.multiple_of((antenna * HALF + number + frame) * KB, KB)
                    turned[pl.ds(place, KB), :] = part[:KB] * twist_a + part[KB:] * twist_b
            return carry

        lax.fori_loop(0, HALF // FG, some_frames, 0, unroll=UN)
        return carry

    lax.fori_loop(0, antennas, one_antenna, 0)

    second = second_ref[...]
    low = jnp.broadcast_to(lane < HALF, (P2, LANES))

    def one_channel(k1, carry):
        for group in range(antennas // 4):
            rows = turned[pl.ds(group * 4 * HALF * KB + k1, 4 * HALF, stride=KB), :]
            spectra = lax.dot_general(
                second, rows.astype(jnp.bfloat16), (((1,), (1,)), ((), ())),
                preferred_element_type=jnp.float32,
            )
            for pair in range(2):
                real = spectra[:P2, pair * LANES:(pair + 1) * LANES]
                imag = spectra[P2:, pair * LANES:(pair + 1) * LANES]
                cosine = cos_ref[group * 2 + pair]
                sine = sin_ref[group * 2 + pair]
                out_real = real * cosine + imag * sine
                out_imag = imag * cosine - real * sine
                antenna = group * 4 + pair * 2
                spread[pl.ds(antenna, P2, stride=antennas), :] = jnp.where(
                    low, out_real, pltpu.roll(out_imag, HALF, 1)
                )
                spread[pl.ds(antenna + 1, P2, stride=antennas), :] = jnp.where(
                    low, pltpu.roll(out_real, HALF, 1), out_imag
                )
        width = P2 // devices
        for step in range(devices):
            target = step ^ me_ref[0]
            place = pl.multiple_of(target * (width * antennas), width * antennas)
            block = spread[pl.ds(place, width * antennas), :].astype(jnp.bfloat16)
            block = block.reshape(width, antennas, LANES)
            outs[step][:, k1] = block
        return carry

    lax.fori_loop(0, KB, one_channel, 0)


def spectra_call(samples, sources, start, rest, me, tables, block, after, carry):
    first, second, twist_a, twist_b, cosine, sine = tables
    antennas = start.shape[0]
    width = P2 // NB
    shape = jax.ShapeDtypeStruct((width, KB, antennas, LANES), jnp.bfloat16)
    grid_spec = pltpu.PrefetchScalarGridSpec(
        num_scalar_prefetch=3,
        grid=(1,),
        in_specs=[pl.BlockSpec(memory_space=pl.ANY) for _ in (*after, *carry, *sources)] + [
            pl.BlockSpec((1, 4 * KB, LANES), lambda i, *_: (block, 0, 0)),
            pl.BlockSpec((2 * P2, 2 * P2), lambda i, *_: (0, 0)),
            pl.BlockSpec((antennas, KB, LANES), lambda i, *_: (0, block, 0)),
            pl.BlockSpec((antennas, KB, LANES), lambda i, *_: (0, block, 0)),
            pl.BlockSpec((antennas // 2, P2, LANES), lambda i, *_: (0, 0, 0)),
            pl.BlockSpec((antennas // 2, P2, LANES), lambda i, *_: (0, 0, 0)),
        ],
        out_specs=[
            pl.BlockSpec((width, KB, antennas, LANES), lambda i, *_: (0, 0, 0, 0))
            for _ in range(NB)
        ] + [pl.BlockSpec(memory_space=pl.ANY) for _ in carry],
        scratch_shapes=[
            pltpu.VMEM((2, RAW_ROWS + STEP_ROWS, LANES), jnp.bfloat16),
            pltpu.VMEM((antennas * HALF * KB, LANES), jnp.float32),
            pltpu.VMEM((P2 * antennas, LANES), jnp.float32),
            pltpu.SemaphoreType.DMA((2, len(sources))),
        ],
    )
    outs = pl.pallas_call(
        functools.partial(spectra_kernel, antennas, sources, len(after), len(carry)),
        grid_spec=grid_spec,
        out_shape=[shape] * NB + [shape] * len(carry),
        input_output_aliases={3 + len(after) + i: NB + i for i in range(len(carry))},
        compiler_params=pltpu.CompilerParams(vmem_limit_bytes=48 << 20),
        cost_estimate=pl.CostEstimate(
            flops=300_000_000_000, bytes_accessed=30_000_000, transcendentals=0
        ),
        name="spectra",
    )(start, rest, me, *after, *carry, *samples, first, second, twist_a, twist_b, cosine, sine)
    return outs[:NB], outs[NB:]


def power_kernel(waits, carried, me_ref, *rest):
    rest = rest[waits + carried:]
    halves = (rest[:NB], rest[NB: 2 * NB])
    out = rest[2 * NB]
    cells, power = rest[2 * NB + 1 + carried:]
    step = pl.program_id(0)
    antennas = BB * NB
    for half in range(2):
        for source in range(NB):
            place = pl.multiple_of((source ^ me_ref[0]) * BB, BB)
            cells[:, pl.ds(place, BB), half * LANES:(half + 1) * LANES] = halves[half][source][0]

    lane = lax.broadcasted_iota(jnp.int32, (antennas, LANES), 1)
    low = lane < HALF

    def swap(value):
        wide = pltpu.roll(value.astype(jnp.float32), HALF, 1)
        return jnp.where(low, wide, -wide).astype(jnp.bfloat16)

    def one_channel(k, carry):
        right = cells[k]
        left = jnp.concatenate(
            [right, jnp.concatenate([swap(right[:, :LANES]), swap(right[:, LANES:])], axis=1)],
            axis=0,
        )
        product = lax.dot_general(
            left, right, (((1,), (1,)), ((), ())), preferred_element_type=jnp.float32
        )
        place = pl.multiple_of((step * KB + k) * (2 * antennas), 2 * antennas)
        power[pl.ds(place, 2 * antennas), :] = product
        return carry

    lax.fori_loop(0, KB, one_channel, 0, unroll=8)

    @pl.when(step == pl.num_programs(0) - 1)
    def _():
        first = 0
        for upper in range(NB):
            def one_row(i, carry):
                for part in range(2):
                    row = part * antennas + upper * BB + i
                    grid = power[pl.ds(row, LANES, stride=2 * antennas), :]
                    turned = jnp.transpose(grid)
                    for lower in range(upper, NB):
                        out[first + lower - upper, part, i] = turned[
                            lower * BB:(lower + 1) * BB
                        ].astype(out.dtype)
                return carry

            lax.fori_loop(0, BB, one_row, 0, unroll=4)
            first += NB - upper


def power_call(me, early, late, dtype, after, carry):
    antennas = BB * NB
    width = P2 // NB
    grid_spec = pltpu.PrefetchScalarGridSpec(
        num_scalar_prefetch=1,
        grid=(width,),
        in_specs=[pl.BlockSpec(memory_space=pl.ANY) for _ in (*after, *carry)] + [
            pl.BlockSpec((1, KB, BB, LANES), lambda i, *_: (i, 0, 0, 0)) for _ in range(2 * NB)
        ],
        out_specs=[pl.BlockSpec((PAIRS, 2, BB, BB, LANES), lambda i, *_: (0, 0, 0, 0, 0))]
        + [pl.BlockSpec(memory_space=pl.ANY) for _ in carry],
        scratch_shapes=[
            pltpu.VMEM((KB, antennas, 2 * LANES), jnp.bfloat16),
            pltpu.VMEM((LANES * 2 * antennas, LANES), jnp.float32),
        ],
    )
    outs = pl.pallas_call(
        functools.partial(power_kernel, len(after), len(carry)),
        grid_spec=grid_spec,
        out_shape=[jax.ShapeDtypeStruct((PAIRS, 2, BB, BB, LANES), dtype)]
        + [jax.ShapeDtypeStruct(piece.shape, piece.dtype) for piece in carry],
        input_output_aliases={1 + len(after) + i: 1 + i for i in range(len(carry))},
        compiler_params=pltpu.CompilerParams(vmem_limit_bytes=54 << 20),
        cost_estimate=pl.CostEstimate(
            flops=300_000_000_000, bytes_accessed=30_000_000, transcendentals=0
        ),
        name="power",
    )(me, *after, *carry, *early, *late)
    return outs[0], outs[1:]


def merge_kernel(factor, *refs):
    pieces, out = refs[:-1], refs[-1]
    values = [ref[...] for ref in pieces[: BLOCKS - 1]]
    last = pieces[BLOCKS - 1][...].astype(jnp.float32)
    for ref in pieces[BLOCKS:]:
        last = last + ref[...].astype(jnp.float32)
    values.append(last)
    values = [value * factor for value in values]
    lane = lax.broadcasted_iota(jnp.int32, values[0].shape, 1)
    per_tile = LANES // P1
    for tile in range(out.shape[1] // LANES):
        total = jnp.zeros_like(values[0])
        for part in range(per_tile):
            for block in range(BLOCKS):
                target = part * P1 + block * KB
                source = (tile * per_tile + part) * KB
                moved = pltpu.roll(values[block], (target - source) % LANES, 1)
                total = jnp.where((lane >= target) & (lane < target + KB), moved, total)
        out[:, tile * LANES:(tile + 1) * LANES] = total


def merge_call(pieces, factor, own):
    rows = own * 2 * BB * BB
    flat = [piece.reshape(rows, LANES) for piece in pieces]
    step = 2 * BB * BB
    channels = (P2 // NB) * P1
    merged = pl.pallas_call(
        functools.partial(merge_kernel, factor),
        grid=(own,),
        in_specs=[pl.BlockSpec((step, LANES), lambda i: (i, 0)) for _ in flat],
        out_specs=pl.BlockSpec((step, channels), lambda i: (i, 0)),
        out_shape=jax.ShapeDtypeStruct((rows, channels), jnp.float32),
        compiler_params=pltpu.CompilerParams(vmem_limit_bytes=32 << 20),
        cost_estimate=pl.CostEstimate(
            flops=1_000_000_000, bytes_accessed=20_000_000, transcendentals=0
        ),
        name="merge",
    )(*flat)
    return merged.reshape(own, 2, BB, BB, channels)


def send(value, step):
    if step == 0:
        return value
    return lax.ppermute(value, "chan", [(i, i ^ step) for i in range(NB)])


def prepare(samples, delays):
    antennas, _, length = samples.shape
    rows = samples.reshape(antennas, 2, length // LANES, LANES).transpose(0, 2, 1, 3)
    rows = rows.reshape(antennas, 2 * length // LANES, LANES)
    delay = delays[:, 0]
    return rows, delay // LANES, delay % LANES


SEND_ORDER = (4, 6, 2, 5, 7, 3, 1, 0)
DEPARTURES = (5, 4, 5, 5, 5, 4, 5, 5, 4, 5, 9)


def fast_body(samples, delays, delay_phase, fringe_rate):
    groups = lax.axis_size("tm")
    rows, start, rest = prepare(samples, delays)
    spill = lax.ppermute(
        rows[:, :SPILL_ROWS], "tm", [(i + 1, i) for i in range(groups - 1)]
    )
    me = lax.axis_index("chan").astype(jnp.int32).reshape(1)
    twist_a, twist_b = twist_tables(delay_phase[:, 1])
    first = jnp.asarray(first_tables(), jnp.bfloat16)
    second = jnp.asarray(second_table(), jnp.bfloat16)
    first_frame = lax.axis_index("tm") * FRAME_COUNT
    tables = [first, second, twist_a, twist_b]
    early_tables = tables + list(fringe_tables(delay_phase, fringe_rate, first_frame))
    late_tables = tables + list(fringe_tables(delay_phase, fringe_rate, first_frame + HALF))

    sources = (
        ((rows,), ((0, RAW_ROWS),), early_tables),
        ((rows, spill), ((ROWS, ROWS), (0, SPILL_ROWS)), late_tables),
    )
    own = PAIRS // groups
    place = lax.axis_index("tm")

    order = [("spectra", 0), ("spectra", 1)]
    for block in range(1, BLOCKS):
        order += [("spectra", 2 * block), ("spectra", 2 * block + 1), ("power", block - 1)]
    order.append(("power", BLOCKS - 1))
    parts = [(half, step) for half in range(2 * BLOCKS) for step in SEND_ORDER if step]
    departs = {}
    queue = list(parts)
    for slot, count in enumerate(DEPARTURES):
        for part in queue[:count]:
            departs[part] = slot
        queue = queue[count:]

    made, got, results = {}, {}, []
    previous = []
    for slot, (kind, number) in enumerate(order):
        waiting = [part for part in parts if departs[part] == slot and part in made]
        carry = [made[part] for part in waiting]
        arrived = [got[part] for part in parts if departs[part] == slot - 2]
        previous = previous + arrived
        if kind == "spectra":
            arrays, spans, half_tables = sources[number % 2]
            pieces, carried = spectra_call(
                arrays, spans, start, rest, me, half_tables, number // 2, previous, carry
            )
            for step in range(NB):
                made[number, step] = pieces[step]
            got[number, 0] = pieces[0]
            previous = [pieces[0]]
        else:
            last = number == BLOCKS - 1
            halves = [[got[2 * number + half, step] for step in range(NB)] for half in range(2)]
            power, carried = power_call(
                me, *halves, jnp.bfloat16 if last else jnp.float32, previous, carry
            )
            previous = [power]
        made.update(zip(waiting, carried))
        for part in parts:
            if departs[part] == slot:
                got[part] = send(made[part], part[1])
        if kind == "power" and not last:
            results.append(lax.psum_scatter(power, "tm", scatter_dimension=0, tiled=True))
    for step in range(groups):
        part = lax.dynamic_slice_in_dim(power, (place ^ step) * own, own, 0)
        if step:
            part = lax.ppermute(part, "tm", [(i, i ^ step) for i in range(groups)])
        results.append(part)
    return merge_call(results, 1.0 / (FRAME_COUNT * groups), own)


def from_behind(value, axis, by):
    devices = lax.axis_size(axis)
    pairs = [(i, i + by) for i in range(devices) if 0 <= i + by < devices]
    return lax.ppermute(value, axis, pairs)


def dft_matrix(length):
    indices = jnp.arange(length, dtype=jnp.int32)
    product = indices[:, None] * indices[None, :] % length
    angle = 2.0 * math.pi / length * product.astype(jnp.float32)
    factor = 1.0 / math.sqrt(length)
    cosine = jnp.cos(angle) * factor
    sine = -jnp.sin(angle) * factor
    upper_half = jnp.concatenate([cosine, sine], axis=1)
    lower_half = jnp.concatenate([-sine, cosine], axis=1)
    return jnp.concatenate([upper_half, lower_half], axis=0).astype(jnp.bfloat16)


def channelize(taper_window):
    batch = taper_window.shape[0]
    frames = taper_window.shape[2]
    first_table = dft_matrix(P1).reshape(2, P1, 2, P1)
    second_table = dft_matrix(P2).reshape(2, P2, 2, P2)
    cells = taper_window.reshape(batch, 2, frames, P1, P2)
    section_one = jnp.einsum(
        "acfmn,cmdk->afdkn", cells, first_table, preferred_element_type=jnp.float32
    )
    product = (
        jnp.arange(P1, dtype=jnp.int32)[:, None]
        * jnp.arange(P2, dtype=jnp.int32)[None, :]
        % CHANNEL_COUNT
    )
    angle = 2.0 * math.pi / CHANNEL_COUNT * product.astype(jnp.float32)
    twist_cos = jnp.cos(angle)
    twist_sin = -jnp.sin(angle)
    real_part = section_one[:, :, 0]
    imag_part = section_one[:, :, 1]
    turned_real = real_part * twist_cos - imag_part * twist_sin
    turned_imag = real_part * twist_sin + imag_part * twist_cos
    turned = jnp.stack([turned_real, turned_imag], axis=2).astype(jnp.bfloat16)
    section_two = jnp.einsum(
        "afdkn,dnem->aefmk", turned, second_table, preferred_element_type=jnp.float32
    )
    return section_two.reshape(batch, 2, frames, CHANNEL_COUNT)


def rotate(spectra, phase_pair, rate, first_frame):
    frames = spectra.shape[2]
    frame_ids = first_frame + jnp.arange(frames, dtype=jnp.int32)
    channels = jnp.arange(CHANNEL_COUNT, dtype=jnp.int32)
    turns = (
        phase_pair[:, 0][:, None, None]
        + rate[:, None, None] * frame_ids[None, :, None]
        + phase_pair[:, 1][:, None, None] * channels[None, None, :]
    ) % CHANNEL_COUNT
    angle = 2.0 * math.pi / CHANNEL_COUNT * turns.astype(jnp.float32)
    cosine = jnp.cos(angle)
    sine = jnp.sin(angle)
    real_part = spectra[:, 0]
    imag_part = spectra[:, 1]
    out_real = real_part * cosine + imag_part * sine
    out_imag = imag_part * cosine - real_part * sine
    return jnp.stack([out_real, out_imag], axis=1).astype(jnp.bfloat16)


def pair_tables(tiles):
    upper_list = []
    lower_list = []
    for upper_tile in range(tiles):
        for lower_tile in range(upper_tile, tiles):
            upper_list.append(upper_tile)
            lower_list.append(lower_tile)
    return (np.array(upper_list, np.int32), np.array(lower_list, np.int32))


def cross_terms(left, right):
    return jnp.einsum("tagh,tbgh->hab", left, right, preferred_element_type=jnp.float32)


def raw_power(stacked):
    real_in = stacked[:, :, 0]
    imag_in = stacked[:, :, 1]
    real_sum = cross_terms(real_in, real_in) + cross_terms(imag_in, imag_in)
    imag_sum = cross_terms(imag_in, real_in) - cross_terms(real_in, imag_in)
    return jnp.stack([real_sum, imag_sum], axis=0)


def cut_pairs(power):
    width = power.shape[1]
    upper_tab, lower_tab = pair_tables(NB)
    blocked = power.reshape(2, width, NB, BB, NB, BB)
    picked_entry = blocked[:, :, upper_tab, :, lower_tab, :]
    return jnp.transpose(picked_entry, (0, 1, 3, 4, 2))


def plain_body(samples, delays, delay_phase, fringe_rate):
    resident_antenna = samples.shape[0]
    block_len = samples.shape[2]
    spill = from_behind(samples[:, :, :DMAX], "tm", -1)
    extended = jnp.concatenate([samples, spill], axis=2)
    taper_window = jax.vmap(
        lambda stream, offset: lax.dynamic_slice_in_dim(stream, offset, block_len, 1)
    )(extended, delays[:, 0])
    taper_window = taper_window.reshape(resident_antenna, 2, FRAME_COUNT, CHANNEL_COUNT)
    spectra = channelize(taper_window)
    rotated = rotate(spectra, delay_phase, fringe_rate, lax.axis_index("tm") * FRAME_COUNT)
    group_total = lax.axis_size("tm")
    factor = 1.0 / (FRAME_COUNT * group_total)
    own_rows = PAIRS // group_total
    channel_major = lax.all_to_all(rotated, "chan", split_axis=3, concat_axis=0, tiled=True)
    all_pairs = cut_pairs(raw_power(channel_major[None])) * factor
    return lax.psum_scatter(
        lax.slice_in_dim(all_pairs, 0, own_rows * lax.axis_size("tm"), axis=0),
        "tm",
        scatter_dimension=0,
        tiled=True,
    )


def body(samples, delays, delay_phase, fringe_rate):
    fits = samples.shape[0] == BB and lax.axis_size("chan") == NB
    whole = samples.shape[2] == FRAME_COUNT * CHANNEL_COUNT and PAIRS % lax.axis_size("tm") == 0
    chosen = fast_body if fits and whole else plain_body
    return chosen(samples, delays, delay_phase, fringe_rate)


def solution(mesh):
    in_specs = (P("chan", None, "tm"), P("chan", "tm"), P("chan", None), P("chan"))
    out_specs = P("tm", None, None, None, "chan")
    return jax.shard_map(body, mesh=mesh, in_specs=in_specs, out_specs=out_specs, check_vma=False)
```

```python
import functools
import math

import jax
import jax.numpy as jnp
import numpy as np
from jax import lax
from jax.experimental import pallas as pl
from jax.experimental.pallas import tpu as pltpu
from jax.sharding import PartitionSpec as P

CHANNEL_COUNT = 4096
P1 = 64
P2 = 64
BB = 16
FRAME_COUNT = 128
NB = 8
PAIRS = 36
DMAX = 32768

LANES = 128
HALF = FRAME_COUNT // 2
ROWS = 2 * HALF * CHANNEL_COUNT // LANES
SPILL_ROWS = 2 * DMAX // LANES
RAW_ROWS = ROWS + SPILL_ROWS
FRAME_ROWS = 2 * CHANNEL_COUNT // LANES
STEP_ROWS = 16
BLOCKS = ((0, 16), (16, 16), (32, 16), (48, 8), (56, 8))
FG = 8
UN = 8


def host_dft(length):
    index = np.arange(length)
    angle = 2.0 * math.pi / length * (np.outer(index, index) % length)
    cosine = np.cos(angle) / math.sqrt(length)
    sine = -np.sin(angle) / math.sqrt(length)
    upper = np.concatenate([cosine, sine], axis=1)
    lower = np.concatenate([-sine, cosine], axis=1)
    return np.concatenate([upper, lower], axis=0).astype(np.float32)


def first_tables(kb):
    table = host_dft(P1).reshape(2, P1 // 2, 2, 2, P1 // kb, kb)
    table = table.transpose(4, 2, 3, 5, 1, 0).reshape(P1 // kb, 4 * kb, P1)
    return np.pad(table, ((0, 0), (0, 0), (0, LANES - P1)))


def second_table():
    return host_dft(P2).T


def turn_factors(turns):
    angle = 2.0 * math.pi / CHANNEL_COUNT * (turns % CHANNEL_COUNT).astype(jnp.float32)
    return jnp.cos(angle), jnp.sin(angle)


def twist_tables(slopes):
    product = np.outer(np.arange(P1), np.arange(P2)) % CHANNEL_COUNT
    angle = 2.0 * math.pi / CHANNEL_COUNT * product
    twist_cos = np.cos(angle).astype(np.float32)
    twist_sin = -np.sin(angle).astype(np.float32)
    cosine, sine = turn_factors(slopes[:, None] * jnp.arange(P1, dtype=jnp.int32)[None, :])
    cosine, sine = cosine[:, :, None], sine[:, :, None]
    real = twist_cos * cosine + twist_sin * sine
    imag = twist_sin * cosine - twist_cos * sine
    return jnp.concatenate([real, imag], axis=2), jnp.concatenate([-imag, real], axis=2)


def fringe_tables(delay_phase, fringe_rate, first_frame):
    antennas = fringe_rate.shape[0]
    frames = first_frame + jnp.arange(HALF, dtype=jnp.int32)
    lanes = delay_phase[:, 0][:, None] + fringe_rate[:, None] * frames[None, :]
    rows = P1 * jnp.arange(P2, dtype=jnp.int32)
    turns = lanes.reshape(antennas // 2, 1, 2, HALF) + (
        delay_phase[:, 1].reshape(antennas // 2, 1, 2, 1) * rows[None, :, None, None]
    )
    return turn_factors(turns.reshape(antennas // 2, P2, 2 * HALF))


def spectra_kernel(
    antennas, kb, sources, waits, carried, start_ref, rest_ref, me_ref, *rest
):
    rest = rest[waits + carried:]
    devices = NB
    sample_refs = rest[: len(sources)]
    first_ref, second_ref, twist_a_ref, twist_b_ref, cos_ref, sin_ref = rest[len(sources):][:6]
    outs = rest[len(sources) + 6:][:devices]
    raw, turned, spread, sems = rest[len(sources) + 6 + devices + carried:]

    def fetches(antenna, slot):
        copies = []
        place = 0
        for number, (begin, count) in enumerate(sources):
            copies.append(pltpu.make_async_copy(
                sample_refs[number].at[antenna, pl.ds(begin, count)],
                raw.at[slot, pl.ds(place, count)],
                sems.at[slot, number],
            ))
            place += count
        return copies

    for copy in fetches(0, 0):
        copy.start()
    raw[:, RAW_ROWS:] = jnp.zeros((2, STEP_ROWS, LANES), raw.dtype)
    lane = lax.broadcasted_iota(jnp.int32, (1, LANES), 1)

    def one_antenna(antenna, carry):
        slot = lax.rem(antenna, 2)

        @pl.when(antenna + 1 < antennas)
        def _():
            for copy in fetches(antenna + 1, 1 - slot):
                copy.start()

        for copy in fetches(antenna, slot):
            copy.wait()
        begin = pl.multiple_of(start_ref[antenna] // (STEP_ROWS // 2) * STEP_ROWS, STEP_ROWS)
        extra = 2 * lax.rem(start_ref[antenna], STEP_ROWS // 2)
        table = first_ref[0].astype(jnp.float32)
        table = jnp.concatenate(
            [pltpu.roll(table, extra, 1), pltpu.roll(table, extra + 2, 1)], axis=0
        ).astype(jnp.bfloat16)[:, :FRAME_ROWS + STEP_ROWS]
        shift = rest_ref[antenna]
        later = jnp.broadcast_to(lane < shift, (4 * kb, LANES))
        odd = jnp.broadcast_to(((lane - shift) & (LANES - 1)) >= P2, (2 * kb, LANES))
        turn_one = (LANES - shift) & (LANES - 1)
        turn_two = (P2 - shift) & (LANES - 1)
        twist_a = twist_a_ref[antenna]
        twist_b = twist_b_ref[antenna]

        def some_frames(step, carry):
            for pair in range(FG // 2):
                number = step * FG + 2 * pair
                row = pl.multiple_of(begin + number * FRAME_ROWS, STEP_ROWS)
                rows = raw[slot, pl.ds(row, 2 * FRAME_ROWS + STEP_ROWS), :]
                both = jnp.concatenate(
                    [rows[:FRAME_ROWS + STEP_ROWS], rows[FRAME_ROWS:]], axis=1
                )
                product = jnp.dot(table, both, preferred_element_type=jnp.float32)
                for frame in range(2):
                    part = product[:, frame * LANES:(frame + 1) * LANES]
                    part = jnp.where(later, part[4 * kb:], part[:4 * kb])
                    part = jnp.where(odd, part[2 * kb:], part[:2 * kb])
                    part = pltpu.roll(part, turn_one, 1) + pltpu.roll(part, turn_two, 1)
                    place = pl.multiple_of((antenna * HALF + number + frame) * kb, kb)
                    turned[pl.ds(place, kb), :] = part[:kb] * twist_a + part[kb:] * twist_b
            return carry

        lax.fori_loop(0, HALF // FG, some_frames, 0, unroll=UN)
        return carry

    lax.fori_loop(0, antennas, one_antenna, 0)

    second = second_ref[...]
    low = jnp.broadcast_to(lane < HALF, (P2, LANES))

    def one_channel(k1, carry):
        for group in range(antennas // 4):
            rows = turned[pl.ds(group * 4 * HALF * kb + k1, 4 * HALF, stride=kb), :]
            spectra = lax.dot_general(
                second, rows.astype(jnp.bfloat16), (((1,), (1,)), ((), ())),
                preferred_element_type=jnp.float32,
            )
            for pair in range(2):
                real = spectra[:P2, pair * LANES:(pair + 1) * LANES]
                imag = spectra[P2:, pair * LANES:(pair + 1) * LANES]
                cosine = cos_ref[group * 2 + pair]
                sine = sin_ref[group * 2 + pair]
                out_real = real * cosine + imag * sine
                out_imag = imag * cosine - real * sine
                antenna = group * 4 + pair * 2
                spread[pl.ds(antenna, P2, stride=antennas), :] = jnp.where(
                    low, out_real, pltpu.roll(out_imag, HALF, 1)
                )
                spread[pl.ds(antenna + 1, P2, stride=antennas), :] = jnp.where(
                    low, pltpu.roll(out_real, HALF, 1), out_imag
                )
        width = P2 // devices
        for step in range(devices):
            target = step ^ me_ref[0]
            place = pl.multiple_of(target * (width * antennas), width * antennas)
            block = spread[pl.ds(place, width * antennas), :].astype(jnp.bfloat16)
            block = block.reshape(width, antennas, LANES)
            outs[step][:, k1] = block
        return carry

    lax.fori_loop(0, kb, one_channel, 0)


def spectra_call(samples, sources, start, rest, me, tables, block, after, carry):
    begin, kb = BLOCKS[block]
    number = begin // kb
    second, twist_a, twist_b, cosine, sine = tables
    first = jnp.asarray(first_tables(kb), jnp.bfloat16)
    antennas = start.shape[0]
    width = P2 // NB
    shape = jax.ShapeDtypeStruct((width, kb, antennas, LANES), jnp.bfloat16)
    grid_spec = pltpu.PrefetchScalarGridSpec(
        num_scalar_prefetch=3,
        grid=(1,),
        in_specs=[pl.BlockSpec(memory_space=pl.ANY) for _ in (*after, *carry, *sources)] + [
            pl.BlockSpec((1, 4 * kb, LANES), lambda i, *_: (number, 0, 0)),
            pl.BlockSpec((2 * P2, 2 * P2), lambda i, *_: (0, 0)),
            pl.BlockSpec((antennas, kb, LANES), lambda i, *_: (0, number, 0)),
            pl.BlockSpec((antennas, kb, LANES), lambda i, *_: (0, number, 0)),
            pl.BlockSpec((antennas // 2, P2, LANES), lambda i, *_: (0, 0, 0)),
            pl.BlockSpec((antennas // 2, P2, LANES), lambda i, *_: (0, 0, 0)),
        ],
        out_specs=[
            pl.BlockSpec((width, kb, antennas, LANES), lambda i, *_: (0, 0, 0, 0))
            for _ in range(NB)
        ] + [pl.BlockSpec(memory_space=pl.ANY) for _ in carry],
        scratch_shapes=[
            pltpu.VMEM((2, RAW_ROWS + STEP_ROWS, LANES), jnp.bfloat16),
            pltpu.VMEM((antennas * HALF * kb, LANES), jnp.float32),
            pltpu.VMEM((P2 * antennas, LANES), jnp.float32),
            pltpu.SemaphoreType.DMA((2, len(sources))),
        ],
    )
    outs = pl.pallas_call(
        functools.partial(spectra_kernel, antennas, kb, sources, len(after), len(carry)),
        grid_spec=grid_spec,
        out_shape=[shape] * NB
        + [jax.ShapeDtypeStruct(piece.shape, piece.dtype) for piece in carry],
        input_output_aliases={3 + len(after) + i: NB + i for i in range(len(carry))},
        compiler_params=pltpu.CompilerParams(vmem_limit_bytes=48 << 20),
        cost_estimate=pl.CostEstimate(
            flops=100_000_000_000, bytes_accessed=30_000_000, transcendentals=0
        ),
        name="spectra",
    )(start, rest, me, *after, *carry, *samples, first, second, twist_a, twist_b, cosine, sine)
    return outs[:NB], outs[NB:]


def power_kernel(kb, waits, carried, me_ref, *rest):
    rest = rest[waits + carried:]
    halves = (rest[:NB], rest[NB: 2 * NB])
    out = rest[2 * NB]
    cells, power = rest[2 * NB + 1 + carried:]
    step = pl.program_id(0)
    antennas = BB * NB
    for half in range(2):
        for source in range(NB):
            place = pl.multiple_of((source ^ me_ref[0]) * BB, BB)
            cells[:, pl.ds(place, BB), half * LANES:(half + 1) * LANES] = halves[half][source][0]

    lane = lax.broadcasted_iota(jnp.int32, (antennas, LANES), 1)
    low = lane < HALF

    def swap(value):
        wide = pltpu.roll(value.astype(jnp.float32), HALF, 1)
        return jnp.where(low, wide, -wide).astype(jnp.bfloat16)

    def one_channel(k, carry):
        right = cells[k]
        left = jnp.concatenate(
            [right, jnp.concatenate([swap(right[:, :LANES]), swap(right[:, LANES:])], axis=1)],
            axis=0,
        )
        product = lax.dot_general(
            left, right, (((1,), (1,)), ((), ())), preferred_element_type=jnp.float32
        )
        place = pl.multiple_of((step * kb + k) * (2 * antennas), 2 * antennas)
        power[pl.ds(place, 2 * antennas), :] = product
        return carry

    lax.fori_loop(0, kb, one_channel, 0, unroll=8)

    channels = (P2 // NB) * kb
    part_rows = BB * channels // LANES

    @pl.when(step == pl.num_programs(0) - 1)
    def _():
        first = 0
        for upper in range(NB):
            def one_row(i, carry):
                for part in range(2):
                    row = part * antennas + upper * BB + i
                    grid = jnp.concatenate([
                        power[pl.ds(row + part_rows * fold, channels, stride=2 * antennas), :]
                        for fold in range(BB // part_rows)
                    ], axis=0)
                    turned = jnp.transpose(grid)
                    for lower in range(upper, NB):
                        out[first + lower - upper, part, i] = turned[
                            lower * BB:(lower + 1) * BB
                        ].astype(out.dtype)
                return carry

            lax.fori_loop(0, part_rows, one_row, 0, unroll=4)
            first += NB - upper


def power_call(me, kb, early, late, dtype, after, carry):
    antennas = BB * NB
    width = P2 // NB
    shape = (PAIRS, 2, BB * width * kb // LANES, BB, LANES)
    grid_spec = pltpu.PrefetchScalarGridSpec(
        num_scalar_prefetch=1,
        grid=(width,),
        in_specs=[pl.BlockSpec(memory_space=pl.ANY) for _ in (*after, *carry)] + [
            pl.BlockSpec((1, kb, BB, LANES), lambda i, *_: (i, 0, 0, 0)) for _ in range(2 * NB)
        ],
        out_specs=[pl.BlockSpec(shape, lambda i, *_: (0, 0, 0, 0, 0))]
        + [pl.BlockSpec(memory_space=pl.ANY) for _ in carry],
        scratch_shapes=[
            pltpu.VMEM((kb, antennas, 2 * LANES), jnp.bfloat16),
            pltpu.VMEM((width * kb * 2 * antennas, LANES), jnp.float32),
        ],
    )
    outs = pl.pallas_call(
        functools.partial(power_kernel, kb, len(after), len(carry)),
        grid_spec=grid_spec,
        out_shape=[jax.ShapeDtypeStruct(shape, dtype)]
        + [jax.ShapeDtypeStruct(piece.shape, piece.dtype) for piece in carry],
        input_output_aliases={1 + len(after) + i: 1 + i for i in range(len(carry))},
        compiler_params=pltpu.CompilerParams(vmem_limit_bytes=54 << 20),
        cost_estimate=pl.CostEstimate(
            flops=100_000_000_000, bytes_accessed=30_000_000, transcendentals=0
        ),
        name="power",
    )(me, *after, *carry, *early, *late)
    return outs[0], outs[1:]


def merge_kernel(factor, counts, *refs):
    out = refs[-1]
    refs = iter(refs[:-1])
    pieces = [[next(refs) for _ in range(count)] for count in counts]
    half = BB * BB // 2
    lane = lax.broadcasted_iota(jnp.int32, (half, LANES), 1)
    per_tile = LANES // P1
    for part in range(2):
        for fold in range(2):
            place = (2 * part + fold) * half
            values = []
            for block, (_, kb) in enumerate(BLOCKS):
                fills = (P2 // NB) * kb == LANES
                rows = slice(place, place + half) if fills else slice(part * half, (part + 1) * half)
                total = pieces[block][0][rows].astype(jnp.float32)
                for ref in pieces[block][1:]:
                    total = total + ref[rows].astype(jnp.float32)
                values.append((total * factor, 0 if fills else fold * (LANES // 2)))
            for tile in range(out.shape[1] // LANES):
                total = jnp.zeros((half, LANES), jnp.float32)
                for run in range(per_tile):
                    for (begin, kb), (value, base) in zip(BLOCKS, values):
                        target = run * P1 + begin
                        source = base + (tile * per_tile + run) * kb
                        moved = pltpu.roll(value, (target - source) % LANES, 1)
                        total = jnp.where((lane >= target) & (lane < target + kb), moved, total)
                out[place:place + half, tile * LANES:(tile + 1) * LANES] = total


def merge_call(pieces, factor, own):
    rows = own * 2 * BB * BB
    flat = [piece.reshape(-1, LANES) for block in pieces for piece in block]
    counts = [len(block) for block in pieces]
    channels = (P2 // NB) * P1
    merged = pl.pallas_call(
        functools.partial(merge_kernel, factor, counts),
        grid=(own,),
        in_specs=[pl.BlockSpec((piece.shape[0] // own, LANES), lambda i: (i, 0)) for piece in flat],
        out_specs=pl.BlockSpec((rows // own, channels), lambda i: (i, 0)),
        out_shape=jax.ShapeDtypeStruct((rows, channels), jnp.float32),
        compiler_params=pltpu.CompilerParams(vmem_limit_bytes=32 << 20),
        cost_estimate=pl.CostEstimate(
            flops=1_000_000_000, bytes_accessed=20_000_000, transcendentals=0
        ),
        name="merge",
    )(*flat)
    return merged.reshape(own, 2, BB, BB, channels)


def send(value, step):
    if step == 0:
        return value
    return lax.ppermute(value, "chan", [(i, i ^ step) for i in range(NB)])


def prepare(samples, delays):
    antennas, _, length = samples.shape
    rows = samples.reshape(antennas, 2, length // LANES, LANES).transpose(0, 2, 1, 3)
    rows = rows.reshape(antennas, 2 * length // LANES, LANES)
    delay = delays[:, 0]
    return rows, delay // LANES, delay % LANES


SEND_ORDER = (4, 6, 2, 5, 7, 3, 1, 0)
DEPARTURES = (5, 4, 5, 5, 5, 4, 5, 5, 4, 6, 6, 5, 6, 5)


def fast_body(samples, delays, delay_phase, fringe_rate):
    groups = lax.axis_size("tm")
    rows, start, rest = prepare(samples, delays)
    spill = lax.ppermute(
        rows[:, :SPILL_ROWS], "tm", [(i + 1, i) for i in range(groups - 1)]
    )
    me = lax.axis_index("chan").astype(jnp.int32).reshape(1)
    twist_a, twist_b = twist_tables(delay_phase[:, 1])
    second = jnp.asarray(second_table(), jnp.bfloat16)
    first_frame = lax.axis_index("tm") * FRAME_COUNT
    tables = [second, twist_a, twist_b]
    early_tables = tables + list(fringe_tables(delay_phase, fringe_rate, first_frame))
    late_tables = tables + list(fringe_tables(delay_phase, fringe_rate, first_frame + HALF))

    sources = (
        ((rows,), ((0, RAW_ROWS),), early_tables),
        ((rows, spill), ((ROWS, ROWS), (0, SPILL_ROWS)), late_tables),
    )
    own = PAIRS // groups
    place = lax.axis_index("tm")

    order = [("spectra", 0), ("spectra", 1)]
    for block in range(1, len(BLOCKS)):
        order += [("spectra", 2 * block), ("spectra", 2 * block + 1), ("power", block - 1)]
    order.append(("power", len(BLOCKS) - 1))
    parts = [(half, step) for half in range(2 * len(BLOCKS)) for step in SEND_ORDER if step]
    departs = {}
    queue = list(parts)
    for slot, count in enumerate(DEPARTURES):
        for part in queue[:count]:
            departs[part] = slot
        queue = queue[count:]

    made, got, results, sums = {}, {}, [], {}
    previous = []
    for slot, (kind, number) in enumerate(order):
        waiting = [part for part in parts if departs[part] == slot and part in made]
        carry = [made[part] for part in waiting]
        arrived = [got[part] for part in parts if departs[part] == slot - 2]
        previous = previous + arrived
        if slot > 3 and sums.get(slot - 4) is not None:
            previous = previous + [sums[slot - 4]]
        if kind == "spectra":
            arrays, spans, half_tables = sources[number % 2]
            pieces, carried = spectra_call(
                arrays, spans, start, rest, me, half_tables, number // 2, previous, carry
            )
            for step in range(NB):
                made[number, step] = pieces[step]
            got[number, 0] = pieces[0]
            previous = [pieces[0]]
        else:
            short = BLOCKS[number][1] < BLOCKS[0][1]
            halves = [[got[2 * number + half, step] for step in range(NB)] for half in range(2)]
            power, carried = power_call(
                me, BLOCKS[number][1], *halves, jnp.bfloat16 if short else jnp.float32, previous, carry
            )
            previous = [power]
        made.update(zip(waiting, carried))
        for part in parts:
            if departs[part] == slot:
                got[part] = send(made[part], part[1])
        if kind == "power" and not short:
            sums[slot] = lax.psum_scatter(power, "tm", scatter_dimension=0, tiled=True)
            results.append([sums[slot]])
        elif kind == "power":
            shares = []
            for step in range(groups):
                share = lax.dynamic_slice_in_dim(power, (place ^ step) * own, own, 0)
                if step:
                    share = lax.ppermute(share, "tm", [(i, i ^ step) for i in range(groups)])
                shares.append(share)
            results.append(shares)
    return merge_call(results, 1.0 / (FRAME_COUNT * groups), own)


def from_behind(value, axis, by):
    devices = lax.axis_size(axis)
    pairs = [(i, i + by) for i in range(devices) if 0 <= i + by < devices]
    return lax.ppermute(value, axis, pairs)


def dft_matrix(length):
    indices = jnp.arange(length, dtype=jnp.int32)
    product = indices[:, None] * indices[None, :] % length
    angle = 2.0 * math.pi / length * product.astype(jnp.float32)
    factor = 1.0 / math.sqrt(length)
    cosine = jnp.cos(angle) * factor
    sine = -jnp.sin(angle) * factor
    upper_half = jnp.concatenate([cosine, sine], axis=1)
    lower_half = jnp.concatenate([-sine, cosine], axis=1)
    return jnp.concatenate([upper_half, lower_half], axis=0).astype(jnp.bfloat16)


def channelize(taper_window):
    batch = taper_window.shape[0]
    frames = taper_window.shape[2]
    first_table = dft_matrix(P1).reshape(2, P1, 2, P1)
    second_table = dft_matrix(P2).reshape(2, P2, 2, P2)
    cells = taper_window.reshape(batch, 2, frames, P1, P2)
    section_one = jnp.einsum(
        "acfmn,cmdk->afdkn", cells, first_table, preferred_element_type=jnp.float32
    )
    product = (
        jnp.arange(P1, dtype=jnp.int32)[:, None]
        * jnp.arange(P2, dtype=jnp.int32)[None, :]
        % CHANNEL_COUNT
    )
    angle = 2.0 * math.pi / CHANNEL_COUNT * product.astype(jnp.float32)
    twist_cos = jnp.cos(angle)
    twist_sin = -jnp.sin(angle)
    real_part = section_one[:, :, 0]
    imag_part = section_one[:, :, 1]
    turned_real = real_part * twist_cos - imag_part * twist_sin
    turned_imag = real_part * twist_sin + imag_part * twist_cos
    turned = jnp.stack([turned_real, turned_imag], axis=2).astype(jnp.bfloat16)
    section_two = jnp.einsum(
        "afdkn,dnem->aefmk", turned, second_table, preferred_element_type=jnp.float32
    )
    return section_two.reshape(batch, 2, frames, CHANNEL_COUNT)


def rotate(spectra, phase_pair, rate, first_frame):
    frames = spectra.shape[2]
    frame_ids = first_frame + jnp.arange(frames, dtype=jnp.int32)
    channels = jnp.arange(CHANNEL_COUNT, dtype=jnp.int32)
    turns = (
        phase_pair[:, 0][:, None, None]
        + rate[:, None, None] * frame_ids[None, :, None]
        + phase_pair[:, 1][:, None, None] * channels[None, None, :]
    ) % CHANNEL_COUNT
    angle = 2.0 * math.pi / CHANNEL_COUNT * turns.astype(jnp.float32)
    cosine = jnp.cos(angle)
    sine = jnp.sin(angle)
    real_part = spectra[:, 0]
    imag_part = spectra[:, 1]
    out_real = real_part * cosine + imag_part * sine
    out_imag = imag_part * cosine - real_part * sine
    return jnp.stack([out_real, out_imag], axis=1).astype(jnp.bfloat16)


def pair_tables(tiles):
    upper_list = []
    lower_list = []
    for upper_tile in range(tiles):
        for lower_tile in range(upper_tile, tiles):
            upper_list.append(upper_tile)
            lower_list.append(lower_tile)
    return (np.array(upper_list, np.int32), np.array(lower_list, np.int32))


def cross_terms(left, right):
    return jnp.einsum("tagh,tbgh->hab", left, right, preferred_element_type=jnp.float32)


def raw_power(stacked):
    real_in = stacked[:, :, 0]
    imag_in = stacked[:, :, 1]
    real_sum = cross_terms(real_in, real_in) + cross_terms(imag_in, imag_in)
    imag_sum = cross_terms(imag_in, real_in) - cross_terms(real_in, imag_in)
    return jnp.stack([real_sum, imag_sum], axis=0)


def cut_pairs(power):
    width = power.shape[1]
    upper_tab, lower_tab = pair_tables(NB)
    blocked = power.reshape(2, width, NB, BB, NB, BB)
    picked_entry = blocked[:, :, upper_tab, :, lower_tab, :]
    return jnp.transpose(picked_entry, (0, 1, 3, 4, 2))


def plain_body(samples, delays, delay_phase, fringe_rate):
    resident_antenna = samples.shape[0]
    block_len = samples.shape[2]
    spill = from_behind(samples[:, :, :DMAX], "tm", -1)
    extended = jnp.concatenate([samples, spill], axis=2)
    taper_window = jax.vmap(
        lambda stream, offset: lax.dynamic_slice_in_dim(stream, offset, block_len, 1)
    )(extended, delays[:, 0])
    taper_window = taper_window.reshape(resident_antenna, 2, FRAME_COUNT, CHANNEL_COUNT)
    spectra = channelize(taper_window)
    rotated = rotate(spectra, delay_phase, fringe_rate, lax.axis_index("tm") * FRAME_COUNT)
    group_total = lax.axis_size("tm")
    factor = 1.0 / (FRAME_COUNT * group_total)
    own_rows = PAIRS // group_total
    channel_major = lax.all_to_all(rotated, "chan", split_axis=3, concat_axis=0, tiled=True)
    all_pairs = cut_pairs(raw_power(channel_major[None])) * factor
    return lax.psum_scatter(
        lax.slice_in_dim(all_pairs, 0, own_rows * lax.axis_size("tm"), axis=0),
        "tm",
        scatter_dimension=0,
        tiled=True,
    )


def body(samples, delays, delay_phase, fringe_rate):
    fits = samples.shape[0] == BB and lax.axis_size("chan") == NB
    whole = samples.shape[2] == FRAME_COUNT * CHANNEL_COUNT and PAIRS % lax.axis_size("tm") == 0
    chosen = fast_body if fits and whole else plain_body
    return chosen(samples, delays, delay_phase, fringe_rate)


def solution(mesh):
    in_specs = (P("chan", None, "tm"), P("chan", "tm"), P("chan", None), P("chan"))
    out_specs = P("tm", None, None, None, "chan")
    return jax.shard_map(body, mesh=mesh, in_specs=in_specs, out_specs=out_specs, check_vma=False)
```

```python
import functools
import math

import jax
import jax.numpy as jnp
import numpy as np
from jax import lax
from jax.experimental import pallas as pl
from jax.experimental.pallas import tpu as pltpu
from jax.sharding import PartitionSpec as P

CHANNEL_COUNT = 4096
P1 = 64
P2 = 64
BB = 16
FRAME_COUNT = 128
NB = 8
PAIRS = 36
DMAX = 32768

LANES = 128
HALF = FRAME_COUNT // 2
ROWS = 2 * HALF * CHANNEL_COUNT // LANES
SPILL_ROWS = 2 * DMAX // LANES
RAW_ROWS = ROWS + SPILL_ROWS
FRAME_ROWS = 2 * CHANNEL_COUNT // LANES
STEP_ROWS = 16
BLOCKS = ((0, 16), (16, 16), (32, 16), (48, 8), (56, 8))
FG = 8
UN = 8


def host_dft(length):
    index = np.arange(length)
    angle = 2.0 * math.pi / length * (np.outer(index, index) % length)
    cosine = np.cos(angle) / math.sqrt(length)
    sine = -np.sin(angle) / math.sqrt(length)
    upper = np.concatenate([cosine, sine], axis=1)
    lower = np.concatenate([-sine, cosine], axis=1)
    return np.concatenate([upper, lower], axis=0).astype(np.float32)


def first_tables(kb):
    table = host_dft(P1).reshape(2, P1 // 2, 2, 2, P1 // kb, kb)
    table = table.transpose(4, 2, 3, 5, 1, 0).reshape(P1 // kb, 4 * kb, P1)
    return np.pad(table, ((0, 0), (0, 0), (0, LANES - P1)))


def second_table():
    return host_dft(P2).T


def turn_factors(turns):
    angle = 2.0 * math.pi / CHANNEL_COUNT * (turns % CHANNEL_COUNT).astype(jnp.float32)
    return jnp.cos(angle), jnp.sin(angle)


def twist_tables(slopes):
    product = np.outer(np.arange(P1), np.arange(P2)) % CHANNEL_COUNT
    angle = 2.0 * math.pi / CHANNEL_COUNT * product
    twist_cos = np.cos(angle).astype(np.float32)
    twist_sin = -np.sin(angle).astype(np.float32)
    cosine, sine = turn_factors(slopes[:, None] * jnp.arange(P1, dtype=jnp.int32)[None, :])
    cosine, sine = cosine[:, :, None], sine[:, :, None]
    real = twist_cos * cosine + twist_sin * sine
    imag = twist_sin * cosine - twist_cos * sine
    return jnp.concatenate([real, imag], axis=2), jnp.concatenate([-imag, real], axis=2)


def fringe_tables(delay_phase, fringe_rate, first_frame):
    antennas = fringe_rate.shape[0]
    frames = first_frame + jnp.arange(HALF, dtype=jnp.int32)
    lanes = delay_phase[:, 0][:, None] + fringe_rate[:, None] * frames[None, :]
    rows = P1 * jnp.arange(P2, dtype=jnp.int32)
    turns = lanes.reshape(antennas // 2, 1, 2, HALF) + (
        delay_phase[:, 1].reshape(antennas // 2, 1, 2, 1) * rows[None, :, None, None]
    )
    return turn_factors(turns.reshape(antennas // 2, P2, 2 * HALF))


def spectra_kernel(
    antennas, kb, sources, waits, carried, start_ref, rest_ref, me_ref, *rest
):
    rest = rest[waits + carried:]
    devices = NB
    sample_refs = rest[: len(sources)]
    first_ref, second_ref, twist_a_ref, twist_b_ref, cos_ref, sin_ref = rest[len(sources):][:6]
    outs = rest[len(sources) + 6:][:devices]
    raw, turned, spread, sems = rest[len(sources) + 6 + devices + carried:]

    def fetches(antenna, slot):
        copies = []
        place = 0
        for number, (begin, count) in enumerate(sources):
            copies.append(pltpu.make_async_copy(
                sample_refs[number].at[antenna, pl.ds(begin, count)],
                raw.at[slot, pl.ds(place, count)],
                sems.at[slot, number],
            ))
            place += count
        return copies

    for copy in fetches(0, 0):
        copy.start()
    raw[:, RAW_ROWS:] = jnp.zeros((2, STEP_ROWS, LANES), raw.dtype)
    lane = lax.broadcasted_iota(jnp.int32, (1, LANES), 1)

    def one_antenna(antenna, carry):
        slot = lax.rem(antenna, 2)

        @pl.when(antenna + 1 < antennas)
        def _():
            for copy in fetches(antenna + 1, 1 - slot):
                copy.start()

        for copy in fetches(antenna, slot):
            copy.wait()
        begin = pl.multiple_of(start_ref[antenna] // (STEP_ROWS // 2) * STEP_ROWS, STEP_ROWS)
        extra = 2 * lax.rem(start_ref[antenna], STEP_ROWS // 2)
        table = first_ref[0].astype(jnp.float32)
        table = jnp.concatenate(
            [pltpu.roll(table, extra, 1), pltpu.roll(table, extra + 2, 1)], axis=0
        ).astype(jnp.bfloat16)[:, :FRAME_ROWS + STEP_ROWS]
        shift = rest_ref[antenna]
        later = jnp.broadcast_to(lane < shift, (4 * kb, LANES))
        odd = jnp.broadcast_to(((lane - shift) & (LANES - 1)) >= P2, (2 * kb, LANES))
        turn_one = (LANES - shift) & (LANES - 1)
        turn_two = (P2 - shift) & (LANES - 1)
        twist_a = twist_a_ref[antenna]
        twist_b = twist_b_ref[antenna]

        def some_frames(step, carry):
            for pair in range(FG // 2):
                number = step * FG + 2 * pair
                row = pl.multiple_of(begin + number * FRAME_ROWS, STEP_ROWS)
                rows = raw[slot, pl.ds(row, 2 * FRAME_ROWS + STEP_ROWS), :]
                both = jnp.concatenate(
                    [rows[:FRAME_ROWS + STEP_ROWS], rows[FRAME_ROWS:]], axis=1
                )
                product = jnp.dot(table, both, preferred_element_type=jnp.float32)
                for frame in range(2):
                    part = product[:, frame * LANES:(frame + 1) * LANES]
                    part = jnp.where(later, part[4 * kb:], part[:4 * kb])
                    part = jnp.where(odd, part[2 * kb:], part[:2 * kb])
                    part = pltpu.roll(part, turn_one, 1) + pltpu.roll(part, turn_two, 1)
                    place = pl.multiple_of((antenna * HALF + number + frame) * kb, kb)
                    turned[pl.ds(place, kb), :] = part[:kb] * twist_a + part[kb:] * twist_b
            return carry

        lax.fori_loop(0, HALF // FG, some_frames, 0, unroll=UN)
        return carry

    lax.fori_loop(0, antennas, one_antenna, 0)

    second = second_ref[...]
    low = jnp.broadcast_to(lane < HALF, (P2, LANES))

    def one_channel(k1, carry):
        for group in range(antennas // 4):
            rows = turned[pl.ds(group * 4 * HALF * kb + k1, 4 * HALF, stride=kb), :]
            spectra = lax.dot_general(
                second, rows.astype(jnp.bfloat16), (((1,), (1,)), ((), ())),
                preferred_element_type=jnp.float32,
            )
            for pair in range(2):
                real = spectra[:P2, pair * LANES:(pair + 1) * LANES]
                imag = spectra[P2:, pair * LANES:(pair + 1) * LANES]
                cosine = cos_ref[group * 2 + pair]
                sine = sin_ref[group * 2 + pair]
                out_real = real * cosine + imag * sine
                out_imag = imag * cosine - real * sine
                antenna = group * 4 + pair * 2
                spread[pl.ds(antenna, P2, stride=antennas), :] = jnp.where(
                    low, out_real, pltpu.roll(out_imag, HALF, 1)
                )
                spread[pl.ds(antenna + 1, P2, stride=antennas), :] = jnp.where(
                    low, pltpu.roll(out_real, HALF, 1), out_imag
                )
        width = P2 // devices
        for step in range(devices):
            target = step ^ me_ref[0]
            place = pl.multiple_of(target * (width * antennas), width * antennas)
            block = spread[pl.ds(place, width * antennas), :].astype(jnp.bfloat16)
            block = block.reshape(width, antennas, LANES)
            outs[step][:, k1] = block
        return carry

    lax.fori_loop(0, kb, one_channel, 0)


def spectra_call(samples, sources, start, rest, me, tables, block, after, carry):
    begin, kb = BLOCKS[block]
    number = begin // kb
    second, twist_a, twist_b, cosine, sine = tables
    first = jnp.asarray(first_tables(kb), jnp.bfloat16)
    antennas = start.shape[0]
    width = P2 // NB
    shape = jax.ShapeDtypeStruct((width, kb, antennas, LANES), jnp.bfloat16)
    grid_spec = pltpu.PrefetchScalarGridSpec(
        num_scalar_prefetch=3,
        grid=(1,),
        in_specs=[pl.BlockSpec(memory_space=pl.ANY) for _ in (*after, *carry, *sources)] + [
            pl.BlockSpec((1, 4 * kb, LANES), lambda i, *_: (number, 0, 0)),
            pl.BlockSpec((2 * P2, 2 * P2), lambda i, *_: (0, 0)),
            pl.BlockSpec((antennas, kb, LANES), lambda i, *_: (0, number, 0)),
            pl.BlockSpec((antennas, kb, LANES), lambda i, *_: (0, number, 0)),
            pl.BlockSpec((antennas // 2, P2, LANES), lambda i, *_: (0, 0, 0)),
            pl.BlockSpec((antennas // 2, P2, LANES), lambda i, *_: (0, 0, 0)),
        ],
        out_specs=[
            pl.BlockSpec((width, kb, antennas, LANES), lambda i, *_: (0, 0, 0, 0))
            for _ in range(NB)
        ] + [pl.BlockSpec(memory_space=pl.ANY) for _ in carry],
        scratch_shapes=[
            pltpu.VMEM((2, RAW_ROWS + STEP_ROWS, LANES), jnp.bfloat16),
            pltpu.VMEM((antennas * HALF * kb, LANES), jnp.float32),
            pltpu.VMEM((P2 * antennas, LANES), jnp.float32),
            pltpu.SemaphoreType.DMA((2, len(sources))),
        ],
    )
    outs = pl.pallas_call(
        functools.partial(spectra_kernel, antennas, kb, sources, len(after), len(carry)),
        grid_spec=grid_spec,
        out_shape=[shape] * NB
        + [jax.ShapeDtypeStruct(piece.shape, piece.dtype) for piece in carry],
        input_output_aliases={3 + len(after) + i: NB + i for i in range(len(carry))},
        compiler_params=pltpu.CompilerParams(vmem_limit_bytes=48 << 20),
        cost_estimate=pl.CostEstimate(
            flops=100_000_000_000, bytes_accessed=30_000_000, transcendentals=0
        ),
        name="spectra",
    )(start, rest, me, *after, *carry, *samples, first, second, twist_a, twist_b, cosine, sine)
    return outs[:NB], outs[NB:]


def power_kernel(kb, waits, carried, me_ref, *rest):
    rest = rest[waits + carried:]
    halves = (rest[:NB], rest[NB: 2 * NB])
    out = rest[2 * NB]
    cells, power = rest[2 * NB + 1 + carried:]
    step = pl.program_id(0)
    antennas = BB * NB
    for half in range(2):
        for source in range(NB):
            place = pl.multiple_of((source ^ me_ref[0]) * BB, BB)
            cells[:, pl.ds(place, BB), half * LANES:(half + 1) * LANES] = halves[half][source][0]

    lane = lax.broadcasted_iota(jnp.int32, (antennas, LANES), 1)
    low = lane < HALF

    def swap(value):
        wide = pltpu.roll(value.astype(jnp.float32), HALF, 1)
        return jnp.where(low, wide, -wide).astype(jnp.bfloat16)

    def one_channel(k, carry):
        right = cells[k]
        left = jnp.concatenate(
            [right, jnp.concatenate([swap(right[:, :LANES]), swap(right[:, LANES:])], axis=1)],
            axis=0,
        )
        product = lax.dot_general(
            left, right, (((1,), (1,)), ((), ())), preferred_element_type=jnp.float32
        )
        place = pl.multiple_of((step * kb + k) * (2 * antennas), 2 * antennas)
        power[pl.ds(place, 2 * antennas), :] = product
        return carry

    lax.fori_loop(0, kb, one_channel, 0, unroll=8)

    channels = (P2 // NB) * kb
    part_rows = BB * channels // LANES

    @pl.when(step == pl.num_programs(0) - 1)
    def _():
        first = 0
        for upper in range(NB):
            def one_row(i, carry):
                for part in range(2):
                    row = part * antennas + upper * BB + i
                    grid = jnp.concatenate([
                        power[pl.ds(row + part_rows * fold, channels, stride=2 * antennas), :]
                        for fold in range(BB // part_rows)
                    ], axis=0)
                    turned = jnp.transpose(grid)
                    for lower in range(upper, NB):
                        out[first + lower - upper, part, i] = turned[
                            lower * BB:(lower + 1) * BB
                        ].astype(out.dtype)
                return carry

            lax.fori_loop(0, part_rows, one_row, 0, unroll=4)
            first += NB - upper


def power_call(me, kb, early, late, dtype, after, carry):
    antennas = BB * NB
    width = P2 // NB
    shape = (PAIRS, 2, BB * width * kb // LANES, BB, LANES)
    grid_spec = pltpu.PrefetchScalarGridSpec(
        num_scalar_prefetch=1,
        grid=(width,),
        in_specs=[pl.BlockSpec(memory_space=pl.ANY) for _ in (*after, *carry)] + [
            pl.BlockSpec((1, kb, BB, LANES), lambda i, *_: (i, 0, 0, 0)) for _ in range(2 * NB)
        ],
        out_specs=[pl.BlockSpec(shape, lambda i, *_: (0, 0, 0, 0, 0))]
        + [pl.BlockSpec(memory_space=pl.ANY) for _ in carry],
        scratch_shapes=[
            pltpu.VMEM((kb, antennas, 2 * LANES), jnp.bfloat16),
            pltpu.VMEM((width * kb * 2 * antennas, LANES), jnp.float32),
        ],
    )
    outs = pl.pallas_call(
        functools.partial(power_kernel, kb, len(after), len(carry)),
        grid_spec=grid_spec,
        out_shape=[jax.ShapeDtypeStruct(shape, dtype)]
        + [jax.ShapeDtypeStruct(piece.shape, piece.dtype) for piece in carry],
        input_output_aliases={1 + len(after) + i: 1 + i for i in range(len(carry))},
        compiler_params=pltpu.CompilerParams(vmem_limit_bytes=54 << 20),
        cost_estimate=pl.CostEstimate(
            flops=100_000_000_000, bytes_accessed=30_000_000, transcendentals=0
        ),
        name="power",
    )(me, *after, *carry, *early, *late)
    return outs[0], outs[1:]


def merge_kernel(factor, counts, *refs):
    out = refs[-1]
    refs = iter(refs[:-1])
    pieces = [[next(refs) for _ in range(count)] for count in counts]
    half = BB * BB // 2
    lane = lax.broadcasted_iota(jnp.int32, (half, LANES), 1)
    per_tile = LANES // P1
    for part in range(2):
        for fold in range(2):
            place = (2 * part + fold) * half
            values = []
            for block, (_, kb) in enumerate(BLOCKS):
                fills = (P2 // NB) * kb == LANES
                rows = slice(place, place + half) if fills else slice(part * half, (part + 1) * half)
                total = pieces[block][0][rows].astype(jnp.float32)
                for ref in pieces[block][1:]:
                    total = total + ref[rows].astype(jnp.float32)
                values.append((total * factor, 0 if fills else fold * (LANES // 2)))
            joined, runs = {}, []
            for tile in range(out.shape[1] // LANES):
                for run in range(per_tile):
                    for (begin, kb), (value, base) in zip(BLOCKS, values):
                        target = run * P1 + begin
                        source = base + (tile * per_tile + run) * kb
                        key = (kb, (target - source) % LANES)
                        here = (lane >= source) & (lane < source + kb)
                        joined[key] = jnp.where(here, value, joined[key]) if key in joined else value
                        runs.append((tile, target, kb, key))
            moved = {key: pltpu.roll(value, key[1], 1) for key, value in joined.items()}
            for tile in range(out.shape[1] // LANES):
                total = jnp.zeros((half, LANES), jnp.float32)
                for place_of, target, kb, key in runs:
                    if place_of == tile:
                        there = (lane >= target) & (lane < target + kb)
                        total = jnp.where(there, moved[key], total)
                out[place:place + half, tile * LANES:(tile + 1) * LANES] = total


def merge_call(pieces, factor, own):
    rows = own * 2 * BB * BB
    flat = [piece.reshape(-1, LANES) for block in pieces for piece in block]
    counts = [len(block) for block in pieces]
    channels = (P2 // NB) * P1
    merged = pl.pallas_call(
        functools.partial(merge_kernel, factor, counts),
        grid=(own,),
        in_specs=[pl.BlockSpec((piece.shape[0] // own, LANES), lambda i: (i, 0)) for piece in flat],
        out_specs=pl.BlockSpec((rows // own, channels), lambda i: (i, 0)),
        out_shape=jax.ShapeDtypeStruct((rows, channels), jnp.float32),
        compiler_params=pltpu.CompilerParams(vmem_limit_bytes=32 << 20),
        cost_estimate=pl.CostEstimate(
            flops=1_000_000_000, bytes_accessed=20_000_000, transcendentals=0
        ),
        name="merge",
    )(*flat)
    return merged.reshape(own, 2, BB, BB, channels)


def send(value, step):
    if step == 0:
        return value
    return lax.ppermute(value, "chan", [(i, i ^ step) for i in range(NB)])


def prepare(samples, delays):
    antennas, _, length = samples.shape
    rows = samples.reshape(antennas, 2, length // LANES, LANES).transpose(0, 2, 1, 3)
    rows = rows.reshape(antennas, 2 * length // LANES, LANES)
    delay = delays[:, 0]
    return rows, delay // LANES, delay % LANES


SEND_ORDER = (4, 6, 2, 5, 7, 3, 1, 0)
DEPARTURES = (5, 4, 5, 5, 5, 4, 5, 5, 4, 6, 6, 5, 6, 5)


def fast_body(samples, delays, delay_phase, fringe_rate):
    groups = lax.axis_size("tm")
    rows, start, rest = prepare(samples, delays)
    spill = lax.ppermute(
        rows[:, :SPILL_ROWS], "tm", [(i + 1, i) for i in range(groups - 1)]
    )
    me = lax.axis_index("chan").astype(jnp.int32).reshape(1)
    twist_a, twist_b = twist_tables(delay_phase[:, 1])
    second = jnp.asarray(second_table(), jnp.bfloat16)
    first_frame = lax.axis_index("tm") * FRAME_COUNT
    tables = [second, twist_a, twist_b]
    early_tables = tables + list(fringe_tables(delay_phase, fringe_rate, first_frame))
    late_tables = tables + list(fringe_tables(delay_phase, fringe_rate, first_frame + HALF))

    sources = (
        ((rows,), ((0, RAW_ROWS),), early_tables),
        ((rows, spill), ((ROWS, ROWS), (0, SPILL_ROWS)), late_tables),
    )
    own = PAIRS // groups
    place = lax.axis_index("tm")

    order = [("spectra", 0), ("spectra", 1)]
    for block in range(1, len(BLOCKS)):
        order += [("spectra", 2 * block), ("spectra", 2 * block + 1), ("power", block - 1)]
    order.append(("power", len(BLOCKS) - 1))
    parts = [(half, step) for half in range(2 * len(BLOCKS)) for step in SEND_ORDER if step]
    departs = {}
    queue = list(parts)
    for slot, count in enumerate(DEPARTURES):
        for part in queue[:count]:
            departs[part] = slot
        queue = queue[count:]

    made, got, results, sums = {}, {}, [], {}
    previous = []
    for slot, (kind, number) in enumerate(order):
        waiting = [part for part in parts if departs[part] == slot and part in made]
        carry = [made[part] for part in waiting]
        arrived = [got[part] for part in parts if departs[part] == slot - 2]
        previous = previous + arrived
        if slot > 3 and sums.get(slot - 4) is not None:
            previous = previous + [sums[slot - 4]]
        if kind == "spectra":
            arrays, spans, half_tables = sources[number % 2]
            pieces, carried = spectra_call(
                arrays, spans, start, rest, me, half_tables, number // 2, previous, carry
            )
            for step in range(NB):
                made[number, step] = pieces[step]
            got[number, 0] = pieces[0]
            previous = [pieces[0]]
        else:
            short = BLOCKS[number][1] < BLOCKS[0][1]
            halves = [[got[2 * number + half, step] for step in range(NB)] for half in range(2)]
            power, carried = power_call(
                me, BLOCKS[number][1], *halves, jnp.bfloat16 if short else jnp.float32, previous, carry
            )
            previous = [power]
        made.update(zip(waiting, carried))
        for part in parts:
            if departs[part] == slot:
                got[part] = send(made[part], part[1])
        if kind == "power" and not short:
            sums[slot] = lax.psum_scatter(power, "tm", scatter_dimension=0, tiled=True)
            results.append([sums[slot]])
        elif kind == "power":
            shares = []
            for step in range(groups):
                share = lax.dynamic_slice_in_dim(power, (place ^ step) * own, own, 0)
                if step:
                    share = lax.ppermute(share, "tm", [(i, i ^ step) for i in range(groups)])
                shares.append(share)
            results.append(shares)
    return merge_call(results, 1.0 / (FRAME_COUNT * groups), own)


def from_behind(value, axis, by):
    devices = lax.axis_size(axis)
    pairs = [(i, i + by) for i in range(devices) if 0 <= i + by < devices]
    return lax.ppermute(value, axis, pairs)


def dft_matrix(length):
    indices = jnp.arange(length, dtype=jnp.int32)
    product = indices[:, None] * indices[None, :] % length
    angle = 2.0 * math.pi / length * product.astype(jnp.float32)
    factor = 1.0 / math.sqrt(length)
    cosine = jnp.cos(angle) * factor
    sine = -jnp.sin(angle) * factor
    upper_half = jnp.concatenate([cosine, sine], axis=1)
    lower_half = jnp.concatenate([-sine, cosine], axis=1)
    return jnp.concatenate([upper_half, lower_half], axis=0).astype(jnp.bfloat16)


def channelize(taper_window):
    batch = taper_window.shape[0]
    frames = taper_window.shape[2]
    first_table = dft_matrix(P1).reshape(2, P1, 2, P1)
    second_table = dft_matrix(P2).reshape(2, P2, 2, P2)
    cells = taper_window.reshape(batch, 2, frames, P1, P2)
    section_one = jnp.einsum(
        "acfmn,cmdk->afdkn", cells, first_table, preferred_element_type=jnp.float32
    )
    product = (
        jnp.arange(P1, dtype=jnp.int32)[:, None]
        * jnp.arange(P2, dtype=jnp.int32)[None, :]
        % CHANNEL_COUNT
    )
    angle = 2.0 * math.pi / CHANNEL_COUNT * product.astype(jnp.float32)
    twist_cos = jnp.cos(angle)
    twist_sin = -jnp.sin(angle)
    real_part = section_one[:, :, 0]
    imag_part = section_one[:, :, 1]
    turned_real = real_part * twist_cos - imag_part * twist_sin
    turned_imag = real_part * twist_sin + imag_part * twist_cos
    turned = jnp.stack([turned_real, turned_imag], axis=2).astype(jnp.bfloat16)
    section_two = jnp.einsum(
        "afdkn,dnem->aefmk", turned, second_table, preferred_element_type=jnp.float32
    )
    return section_two.reshape(batch, 2, frames, CHANNEL_COUNT)


def rotate(spectra, phase_pair, rate, first_frame):
    frames = spectra.shape[2]
    frame_ids = first_frame + jnp.arange(frames, dtype=jnp.int32)
    channels = jnp.arange(CHANNEL_COUNT, dtype=jnp.int32)
    turns = (
        phase_pair[:, 0][:, None, None]
        + rate[:, None, None] * frame_ids[None, :, None]
        + phase_pair[:, 1][:, None, None] * channels[None, None, :]
    ) % CHANNEL_COUNT
    angle = 2.0 * math.pi / CHANNEL_COUNT * turns.astype(jnp.float32)
    cosine = jnp.cos(angle)
    sine = jnp.sin(angle)
    real_part = spectra[:, 0]
    imag_part = spectra[:, 1]
    out_real = real_part * cosine + imag_part * sine
    out_imag = imag_part * cosine - real_part * sine
    return jnp.stack([out_real, out_imag], axis=1).astype(jnp.bfloat16)


def pair_tables(tiles):
    upper_list = []
    lower_list = []
    for upper_tile in range(tiles):
        for lower_tile in range(upper_tile, tiles):
            upper_list.append(upper_tile)
            lower_list.append(lower_tile)
    return (np.array(upper_list, np.int32), np.array(lower_list, np.int32))


def cross_terms(left, right):
    return jnp.einsum("tagh,tbgh->hab", left, right, preferred_element_type=jnp.float32)


def raw_power(stacked):
    real_in = stacked[:, :, 0]
    imag_in = stacked[:, :, 1]
    real_sum = cross_terms(real_in, real_in) + cross_terms(imag_in, imag_in)
    imag_sum = cross_terms(imag_in, real_in) - cross_terms(real_in, imag_in)
    return jnp.stack([real_sum, imag_sum], axis=0)


def cut_pairs(power):
    width = power.shape[1]
    upper_tab, lower_tab = pair_tables(NB)
    blocked = power.reshape(2, width, NB, BB, NB, BB)
    picked_entry = blocked[:, :, upper_tab, :, lower_tab, :]
    return jnp.transpose(picked_entry, (0, 1, 3, 4, 2))


def plain_body(samples, delays, delay_phase, fringe_rate):
    resident_antenna = samples.shape[0]
    block_len = samples.shape[2]
    spill = from_behind(samples[:, :, :DMAX], "tm", -1)
    extended = jnp.concatenate([samples, spill], axis=2)
    taper_window = jax.vmap(
        lambda stream, offset: lax.dynamic_slice_in_dim(stream, offset, block_len, 1)
    )(extended, delays[:, 0])
    taper_window = taper_window.reshape(resident_antenna, 2, FRAME_COUNT, CHANNEL_COUNT)
    spectra = channelize(taper_window)
    rotated = rotate(spectra, delay_phase, fringe_rate, lax.axis_index("tm") * FRAME_COUNT)
    group_total = lax.axis_size("tm")
    factor = 1.0 / (FRAME_COUNT * group_total)
    own_rows = PAIRS // group_total
    channel_major = lax.all_to_all(rotated, "chan", split_axis=3, concat_axis=0, tiled=True)
    all_pairs = cut_pairs(raw_power(channel_major[None])) * factor
    return lax.psum_scatter(
        lax.slice_in_dim(all_pairs, 0, own_rows * lax.axis_size("tm"), axis=0),
        "tm",
        scatter_dimension=0,
        tiled=True,
    )


def body(samples, delays, delay_phase, fringe_rate):
    fits = samples.shape[0] == BB and lax.axis_size("chan") == NB
    whole = samples.shape[2] == FRAME_COUNT * CHANNEL_COUNT and PAIRS % lax.axis_size("tm") == 0
    chosen = fast_body if fits and whole else plain_body
    return chosen(samples, delays, delay_phase, fringe_rate)


def solution(mesh):
    in_specs = (P("chan", None, "tm"), P("chan", "tm"), P("chan", None), P("chan"))
    out_specs = P("tm", None, None, None, "chan")
    return jax.shard_map(body, mesh=mesh, in_specs=in_specs, out_specs=out_specs, check_vma=False)
```
